32 devices in a mesh: loop: 8 (over y, x, core), dp: 4 (over z).
Axes of the slice: x: 2, y: 2, z: 4, core: 2. Of those that a mesh axis runs over, the one named last changes fastest.
Arguments:
- image_raw: bfloat16 [4, 1024, 1152], P('dp', 'loop'), may hold values from -0.19921875 to 0.19921875
- text_feat: bfloat16 [4, 1024, 1152], P('dp', 'loop'), may hold values from -6 to 6
- text_head: bfloat16 [1152, 1152], replicated, may hold values from -0.1875 to 0.1875
- image_of_pair: int32 [4, 1024], P('dp', 'loop'), may hold values from 0 to 255, as said below
- logit_scale: float32 [], replicated, may hold values from 10 to 30
- logit_bias: float32 [], replicated, may hold values from -3 to -1
Outputs:
- d_text_feat: float32 [4, 1024, 1152], P('dp', 'loop')
- d_image: float32 [8, 256, 1152], P('loop', 'dp')
The draws below stay inside these ranges and needn't reach their ends.
Inputs may be any that keep to these rules, and one draw needn't show every extreme that they name: `image_of_pair`: pair row i of a replica belongs to column i // 128. Every image of a column is named by 1 to 5 pairs of that column over all replicas. Image m of a column is owned by the device of that column's loop index and dp index m // 64. The pairs of one device name images of one owner at most 80 times; in every draw some owner receives exactly 80 from every device of its column.
All inputs are finite; a program needn't handle non-finite values.
Results may differ from the reference program's by a relative error of at most 0.0057.
Values may be sent and summed in bfloat16 or wider, within the bound.
A program may use at most 64 MiB of HBM per device.

```python
import math
import jax
import jax.numpy as jnp
from jax import lax

D = 1152
E = 1152
PAIR_DEV = 128
IMG_DEV = 64
REPLICAS = 4
COLUMNS = 8
ROWS = 1024
POOL = 1024
IMG_COL = 256


def column_images(key):
    k_owner, k_heavy, k_light, k_first, k_second, k_device = jax.random.split(key, 6)
    heavy_owners = REPLICAS // 4
    quads = heavy_owners * IMG_DEV
    order = jax.random.permutation(k_owner, REPLICAS)
    owner_rank = jnp.argsort(order).astype(jnp.int32)
    heavy = jax.random.randint(k_heavy, (quads,), 3, 6)
    heavy = jnp.where(jnp.arange(quads) < IMG_DEV, 5, heavy).astype(jnp.int32)
    extra = 5 - heavy
    first = jax.random.randint(k_first, (quads,), 0, 3)
    second = jax.random.randint(k_second, (quads,), 0, 3)
    places = jnp.arange(3)[None, :]
    light = 1 + ((places == first[:, None]) & (extra[:, None] >= 1)).astype(jnp.int32)
    light = light + ((places == second[:, None]) & (extra[:, None] >= 2)).astype(jnp.int32)
    light_order = jax.random.permutation(k_light, 3 * quads)
    light_flat = light.reshape(-1)[light_order]
    images = jnp.arange(IMG_COL)
    rank = owner_rank[images // IMG_DEV]
    within = images % IMG_DEV
    heavy_index = jnp.clip(rank * IMG_DEV + within, 0, quads - 1)
    light_index = jnp.clip((rank - heavy_owners) * IMG_DEV + within, 0, 3 * quads - 1)
    counts = jnp.where(rank < heavy_owners, heavy[heavy_index], light_flat[light_index])
    ends = jnp.cumsum(counts)
    total = REPLICAS * PAIR_DEV
    caption = jnp.arange(total)
    image_of_caption = jnp.sum((ends[None, :] <= caption[:, None]).astype(jnp.int32), axis=1)
    sender = caption // 2 % REPLICAS
    slot = caption // (2 * REPLICAS) * 2 + caption % 2
    grid = jnp.zeros((REPLICAS, PAIR_DEV), jnp.int32).at[sender, slot].set(image_of_caption.astype(jnp.int32))
    device_keys = jax.random.split(k_device, REPLICAS)
    shuffles = jax.vmap(lambda k: jax.random.permutation(k, PAIR_DEV))(device_keys)
    return jnp.take_along_axis(grid, shuffles, axis=1)


def draw_image_of_pair(key, part):
    key = jax.random.fold_in(key, 11)
    column_keys = jax.random.split(key, COLUMNS)
    columns = jax.vmap(column_images)(column_keys)
    return jnp.transpose(columns, (1, 0, 2)).reshape(REPLICAS, ROWS).astype(jnp.int32)


def level_of(key, dims, cuts, least, largest):
    def one(axis_at, blocks):
        steps = jax.random.uniform(jax.random.fold_in(jax.random.fold_in(key, 6), axis_at), (blocks,), jnp.float32, least / len(cuts), largest / len(cuts))
        return jnp.repeat(jnp.exp(steps), dims[axis_at] // blocks).reshape((-1,) + (1,) * (len(dims) - axis_at - 1))

    loudness = one(*cuts[0])
    for cut in cuts[1:]:
        loudness = loudness * one(*cut)
    return loudness


def gaussian(key, dims, width, reach, cuts=(), kind=jnp.bfloat16):
    result = jax.random.normal(key, dims, jnp.float32) * width
    if len(cuts) > 0:
        result = level_of(key, dims, cuts, -0.22, 0.18) * result
    return jnp.clip(result, min=-reach, max=reach).astype(kind)


def setup_inputs(seed: int = 0) -> dict:
    splits = jax.random.split(jax.random.key(seed), 7)
    return {
        "image_raw": gaussian(splits[0], (REPLICAS, ROWS, E), 0.03, 0.19921875, ((0, 4), (1, 8))),
        "text_feat": gaussian(splits[1], (REPLICAS, ROWS, D), 1.0, 6.0, ((0, 4), (1, 8))),
        "text_head": gaussian(splits[2], (D, E), D ** -0.5, 0.1875),
        "image_of_pair": draw_image_of_pair(jax.random.fold_in(splits[6], 71), 0),
        "logit_scale": jnp.clip(jnp.exp(jax.random.uniform(splits[4], (), jnp.float32, math.log(10.0), math.log(30.0))), 10.0, 30.0),
        "logit_bias": jnp.clip(jax.random.uniform(splits[5], (), jnp.float32, -3.0, -1.0), -3.0, -1.0),
    }


EPS = 1e-06

def unit_rows(values):
    inv = lax.rsqrt(lax.optimization_barrier(jnp.sum(values * values, axis=-1, keepdims=True)) + EPS)
    return (values * inv, inv)

def reference(image_raw, text_feat, text_head, image_of_pair, logit_scale, logit_bias):
    unit_x, inv_x = unit_rows(image_raw.astype(jnp.float32))
    image_emb = unit_x.astype(jnp.bfloat16)
    text_pre = jnp.dot(text_feat.reshape(REPLICAS * ROWS, D), text_head, preferred_element_type=jnp.float32)
    unit_y, inv_y = unit_rows(text_pre.reshape(REPLICAS, ROWS, E))
    text_emb = unit_y.astype(jnp.bfloat16)
    pools_all = REPLICAS * (ROWS // POOL)
    column = jnp.arange(POOL, dtype=jnp.int32) // PAIR_DEV

    def pool_grads(items):
        x_block, y_block, labels = items
        same = (column[:, None] == column[None, :]) & (labels[:, None] == labels[None, :])
        logits = logit_scale * jnp.dot(x_block, y_block.T, preferred_element_type=jnp.float32) + logit_bias
        sign = jnp.where(same, jnp.float32(1.0), jnp.float32(-1.0))
        weight = (-sign * jax.nn.sigmoid(-sign * logits)).astype(jnp.bfloat16)
        d_img = logit_scale * jnp.dot(weight, y_block, preferred_element_type=jnp.float32)
        d_txt = logit_scale * jnp.dot(weight.T, x_block, preferred_element_type=jnp.float32)
        return (d_img, d_txt)
    d_img_emb, d_txt_emb = lax.map(pool_grads, (image_emb.reshape(pools_all, POOL, E), text_emb.reshape(pools_all, POOL, E), image_of_pair.reshape(pools_all, POOL)))
    d_img_emb = d_img_emb.reshape(REPLICAS, ROWS, E)
    d_txt_emb = d_txt_emb.reshape(REPLICAS, ROWS, E)
    d_image_pair = (d_img_emb - unit_x * lax.optimization_barrier(jnp.sum(unit_x * d_img_emb, axis=-1, keepdims=True))) * inv_x
    d_text_pre = ((d_txt_emb - unit_y * lax.optimization_barrier(jnp.sum(unit_y * d_txt_emb, axis=-1, keepdims=True))) * inv_y).astype(jnp.bfloat16)
    d_text_feat = jnp.dot(d_text_pre.reshape(REPLICAS * ROWS, E), text_head.T, preferred_element_type=jnp.float32)
    row_column = jnp.arange(ROWS, dtype=jnp.int32) // PAIR_DEV
    segment = (row_column[None, :] * IMG_COL + image_of_pair).astype(jnp.int32)
    d_image = jax.ops.segment_sum(d_image_pair.reshape(REPLICAS * ROWS, E), segment.reshape(-1), num_segments=COLUMNS * IMG_COL)
    return (d_text_feat.reshape(REPLICAS, ROWS, D), d_image.reshape(COLUMNS, IMG_COL, E))
```

```python
import functools

import jax
import jax.numpy as jnp
from jax import lax
from jax.experimental import pallas as pl
from jax.experimental.pallas import tpu as pltpu
from jax.sharding import PartitionSpec as P

EPS = 1e-06
POOL_DEVS = 8
CORE, NEAR, FAR = 1, 2, 4
NT = (((1,), (1,)), ((), ()))


def partner(me, mask):
    bit = lax.rem(lax.div(me, mask), 2)
    return me + mask * (1 - 2 * bit)


class Spread:
    def __init__(self, buf, send, recv, me, rows):
        half = rows // 2
        peers = {m: partner(me, m) for m in (CORE, NEAR, FAR)}

        def copy(at, slot, mask, first, count):
            source = buf.at[pl.ds(slot * rows + first, count)]
            target = buf.at[pl.ds((slot ^ mask) * rows + first, count)]
            return pltpu.make_async_remote_copy(
                src_ref=source,
                dst_ref=target,
                send_sem=send.at[at],
                recv_sem=recv.at[at],
                device_id={"loop": peers[mask]},
                device_id_type=pl.DeviceIdType.MESH,
            )

        self.own_core = copy(0, 0, CORE, 0, rows)
        self.near_a = copy(1, 0, NEAR, 0, half)
        self.near_b = copy(2, 0, NEAR, half, half)
        self.far_a = copy(3, 0, FAR, 0, half)
        self.far_b = copy(4, 0, FAR, half, half)
        self.diag_a = copy(5, NEAR, FAR, 0, half)
        self.diag_b = copy(6, FAR, NEAR, half, half)
        self.near_core = copy(7, NEAR, CORE, 0, rows)
        self.far_core = copy(8, FAR, CORE, 0, rows)
        self.diag_core_a = copy(9, NEAR | FAR, CORE, 0, half)
        self.diag_core_b = copy(10, NEAR | FAR, CORE, half, half)


COPIES = 11


def kernel(
    owners,
    scale_ref,
    shift_ref,
    label_ref,
    image_ref,
    feat_ref,
    head_ref,
    d_feat_ref,
    d_image_ref,
    image_v,
    feat_v,
    head_v,
    xbuf,
    ybuf,
    unit_y_v,
    d_pair_v,
    d_feat_v,
    table_out,
    table_in,
    load_sem,
    store_sem,
    x_send,
    x_recv,
    y_send,
    y_recv,
    t_send,
    t_recv,
):
    rows, width = image_v.shape
    images = table_out.shape[1]
    me = lax.axis_index("loop")
    owner = lax.axis_index("dp")

    load_image = pltpu.make_async_copy(image_ref.at[0], image_v, load_sem.at[0])
    load_feat = pltpu.make_async_copy(feat_ref.at[0], feat_v, load_sem.at[1])
    load_head = pltpu.make_async_copy(head_ref, head_v, load_sem.at[2])
    load_image.start()
    load_feat.start()
    load_head.start()

    barrier = pltpu.get_barrier_semaphore()
    for mask in (CORE, NEAR, FAR):
        pl.semaphore_signal(
            barrier, inc=1, device_id={"loop": partner(me, mask)}, device_id_type=pl.DeviceIdType.MESH
        )
    for apart in range(1, owners):
        pl.semaphore_signal(
            barrier,
            inc=1,
            device_id={"dp": lax.rem(owner + apart, owners)},
            device_id_type=pl.DeviceIdType.MESH,
        )

    scale = scale_ref[0]
    shift = shift_ref[0]
    label_row = label_ref[...].astype(jnp.float32)
    label_grid = jnp.broadcast_to(label_row, (rows, rows))
    same = label_grid == label_grid.T

    xs = Spread(xbuf, x_send, x_recv, me, rows)
    ys = Spread(ybuf, y_send, y_recv, me, rows)

    load_image.wait()
    image = image_v[...].astype(jnp.float32)
    inv_x = lax.rsqrt(jnp.sum(image * image, axis=-1, keepdims=True) + EPS)
    xbuf[pl.ds(0, rows)] = (image * inv_x).astype(jnp.bfloat16)

    pl.semaphore_wait(barrier, 3 + owners - 1)
    xs.near_a.start()
    xs.far_b.start()
    xs.own_core.start()

    load_feat.wait()
    load_head.wait()
    text_pre = jnp.dot(feat_v[...], head_v[...], preferred_element_type=jnp.float32)
    inv_y = lax.rsqrt(jnp.sum(text_pre * text_pre, axis=-1, keepdims=True) + EPS)
    unit_y = text_pre * inv_y
    unit_y_v[...] = unit_y
    ybuf[pl.ds(0, rows)] = unit_y.astype(jnp.bfloat16)
    ys.near_a.start()
    ys.far_b.start()
    ys.near_b.start()
    ys.far_a.start()
    ys.own_core.start()

    def part(mine, buf, group):
        block = buf[pl.ds(group * 2 * rows, 2 * rows)]
        logits = scale * lax.dot_general(mine, block, NT, preferred_element_type=jnp.float32) + shift
        if group == 0:
            flip = jnp.concatenate([same, jnp.zeros_like(same)], axis=1)
            value = jax.nn.sigmoid(jnp.where(flip, -logits, logits))
            value = jnp.where(flip, -value, value)
        else:
            value = jax.nn.sigmoid(logits)
        return jnp.dot(value.astype(jnp.bfloat16), block, preferred_element_type=jnp.float32)

    x_own = xbuf[pl.ds(0, rows)]
    y_own = ybuf[pl.ds(0, rows)]

    ys.own_core.wait_recv()
    total = part(x_own, ybuf, 0)
    ys.near_a.wait_recv()
    ys.diag_a.start()
    ys.far_b.wait_recv()
    ys.diag_b.start()
    ys.near_b.wait_recv()
    ys.near_core.start()
    ys.far_a.wait_recv()
    ys.far_core.start()
    ys.diag_a.wait_send()
    ys.diag_b.wait_send()
    xs.near_b.start()
    xs.far_a.start()
    xs.near_a.wait_recv()
    xs.diag_a.start()
    xs.far_b.wait_recv()
    xs.diag_b.start()
    ys.near_core.wait_recv()
    total = total + part(x_own, ybuf, 1)
    ys.far_core.wait_recv()
    total = total + part(x_own, ybuf, 2)
    ys.diag_a.wait_recv()
    ys.diag_core_a.start()
    ys.diag_b.wait_recv()
    ys.diag_core_b.start()
    ys.diag_core_a.wait_recv()
    ys.diag_core_b.wait_recv()
    total = total + part(x_own, ybuf, 3)
    grad = scale * total
    unit_x = image * inv_x
    d_pair = (grad - unit_x * jnp.sum(unit_x * grad, axis=-1, keepdims=True)) * inv_x
    d_pair_v[...] = d_pair.astype(jnp.bfloat16)

    def table(apart):
        first = (lax.rem(owner + apart, owners) * images).astype(jnp.float32)
        ids = lax.broadcasted_iota(jnp.int32, (images, rows), 0).astype(jnp.float32) + first
        onehot = jnp.where(ids == label_row, 1.0, 0.0).astype(jnp.bfloat16)
        return jnp.dot(onehot, d_pair_v[...], preferred_element_type=jnp.float32)

    tables = []
    order = sorted(range(1, owners), key=lambda apart: (-min(apart, owners - apart), apart))
    for apart in order:
        table_out[apart] = table(apart).astype(jnp.bfloat16)
        send = pltpu.make_async_remote_copy(
            src_ref=table_out.at[apart],
            dst_ref=table_in.at[apart],
            send_sem=t_send.at[apart],
            recv_sem=t_recv.at[apart],
            device_id={"dp": lax.rem(owner + apart, owners)},
            device_id_type=pl.DeviceIdType.MESH,
        )
        send.start()
        tables.append((apart, send))
    d_image_ref[0] = table(0)

    xs.near_b.wait_recv()
    xs.near_core.start()
    xs.far_a.wait_recv()
    xs.far_core.start()
    xs.own_core.wait_recv()
    total = part(y_own, xbuf, 0)
    xs.near_core.wait_recv()
    total = total + part(y_own, xbuf, 1)
    xs.far_core.wait_recv()
    total = total + part(y_own, xbuf, 2)
    xs.diag_a.wait_recv()
    xs.diag_core_a.start()
    xs.diag_b.wait_recv()
    xs.diag_core_b.start()
    xs.diag_core_a.wait_recv()
    xs.diag_core_b.wait_recv()
    total = total + part(y_own, xbuf, 3)
    grad = scale * total
    unit_y = unit_y_v[...]
    d_text = (grad - unit_y * jnp.sum(unit_y * grad, axis=-1, keepdims=True)) * inv_y
    d_feat_v[...] = lax.dot_general(
        d_text.astype(jnp.bfloat16), head_v[...], NT, preferred_element_type=jnp.float32
    )
    store = pltpu.make_async_copy(d_feat_v, d_feat_ref.at[0], store_sem)
    store.start()

    for apart, send in tables:
        send.wait_recv()
        d_image_ref[0] += table_in[apart].astype(jnp.float32)

    store.wait()
    for spread in (xs, ys):
        for name, copy in vars(spread).items():
            if spread is xs or name not in ("diag_a", "diag_b"):
                copy.wait_send()
    for _, send in tables:
        send.wait_send()


def shards(owners, image_raw, text_feat, text_head, image_of_pair, logit_scale, logit_bias):
    _, rows, width = image_raw.shape
    depth = text_head.shape[0]
    images = rows // 2
    anywhere = pl.BlockSpec(memory_space=pl.ANY)
    scalar = pl.BlockSpec(memory_space=pltpu.SMEM)
    vmem = pl.BlockSpec(memory_space=pltpu.VMEM)
    dma = pltpu.SemaphoreType.DMA
    return pl.pallas_call(
        functools.partial(kernel, owners),
        out_shape=(
            jax.ShapeDtypeStruct((1, rows, depth), jnp.float32),
            jax.ShapeDtypeStruct((1, images, width), jnp.float32),
        ),
        in_specs=[scalar, scalar, vmem, anywhere, anywhere, anywhere],
        out_specs=(anywhere, vmem),
        scratch_shapes=[
            pltpu.VMEM((rows, width), jnp.bfloat16),
            pltpu.VMEM((rows, depth), jnp.bfloat16),
            pltpu.VMEM((depth, width), jnp.bfloat16),
            pltpu.VMEM((POOL_DEVS * rows, width), jnp.bfloat16),
            pltpu.VMEM((POOL_DEVS * rows, width), jnp.bfloat16),
            pltpu.VMEM((rows, width), jnp.float32),
            pltpu.VMEM((rows, width), jnp.bfloat16),
            pltpu.VMEM((rows, depth), jnp.float32),
            pltpu.VMEM((owners, images, width), jnp.bfloat16),
            pltpu.VMEM((owners, images, width), jnp.bfloat16),
            dma((3,)),
            dma,
            dma((COPIES,)),
            dma((COPIES,)),
            dma((COPIES,)),
            dma((COPIES,)),
            dma((owners,)),
            dma((owners,)),
        ],
        compiler_params=pltpu.CompilerParams(
            collective_id=0, has_side_effects=True, vmem_limit_bytes=48 * 1024 * 1024
        ),
    )(
        logit_scale.reshape((1,)),
        logit_bias.reshape((1,)),
        image_of_pair,
        image_raw,
        text_feat,
        text_head,
    )


def solution(mesh):
    placed = (P("dp", "loop", None), P("dp", "loop", None), P(), P("dp", "loop"), P(), P())
    return jax.shard_map(
        functools.partial(shards, mesh.shape["dp"]),
        mesh=mesh,
        in_specs=placed,
        out_specs=(P("dp", "loop", None), P("loop", "dp", None)),
        check_vma=False,
    )
```

```python
import functools

import jax
import jax.numpy as jnp
from jax import lax
from jax.experimental import pallas as pl
from jax.experimental.pallas import tpu as pltpu
from jax.sharding import PartitionSpec as P

EPS = 1e-06
POOL_DEVS = 8
CORE, NEAR, FAR = 1, 2, 4
NT = (((1,), (1,)), ((), ()))


def partner(me, mask):
    bit = lax.rem(lax.div(me, mask), 2)
    return me + mask * (1 - 2 * bit)


class Spread:
    def __init__(self, buf, send, recv, me, rows):
        half = rows // 2
        peers = {m: partner(me, m) for m in (CORE, NEAR, FAR)}

        def copy(at, slot, mask, first, count):
            source = buf.at[pl.ds(slot * rows + first, count)]
            target = buf.at[pl.ds((slot ^ mask) * rows + first, count)]
            return pltpu.make_async_remote_copy(
                src_ref=source,
                dst_ref=target,
                send_sem=send.at[at],
                recv_sem=recv.at[at],
                device_id={"loop": peers[mask]},
                device_id_type=pl.DeviceIdType.MESH,
            )

        self.own_core = copy(0, 0, CORE, 0, rows)
        self.near_a = copy(1, 0, NEAR, 0, half)
        self.near_b = copy(2, 0, NEAR, half, half)
        self.far_a = copy(3, 0, FAR, 0, half)
        self.far_b = copy(4, 0, FAR, half, half)
        self.near_core = copy(5, NEAR, CORE, 0, rows)
        self.far_core = copy(6, FAR, CORE, 0, rows)
        piece = half // 2
        self.diag_a = [copy(7 + i, NEAR, FAR, i * piece, piece) for i in range(2)]
        self.diag_b = [copy(9 + i, FAR, NEAR, half + i * piece, piece) for i in range(2)]
        diag = NEAR | FAR
        self.diag_core_a = [copy(11 + i, diag, CORE, i * piece, piece) for i in range(2)]
        self.diag_core_b = [copy(13 + i, diag, CORE, half + i * piece, piece) for i in range(2)]

    def forward(self):
        self.near_a.wait_recv()
        for c in self.diag_a:
            c.start()
        self.far_b.wait_recv()
        for c in self.diag_b:
            c.start()

    def relay_diag(self):
        for i in range(2):
            self.diag_a[i].wait_recv()
            self.diag_core_a[i].start()
            self.diag_b[i].wait_recv()
            self.diag_core_b[i].start()

    def await_diag_core(self):
        for c in self.diag_core_a + self.diag_core_b:
            c.wait_recv()

    def drain(self, diag):
        for c in (self.own_core, self.near_a, self.near_b, self.far_a, self.far_b, self.near_core, self.far_core):
            c.wait_send()
        for c in self.diag_core_a + self.diag_core_b:
            c.wait_send()
        if diag:
            self.drain_diag()

    def drain_diag(self):
        for c in self.diag_a + self.diag_b:
            c.wait_send()


COPIES = 15


class Line:
    def __init__(self, refs, owner, label_row, width, piece_ends):
        self.label_out, self.label_in, self.pair_in, self.table_out, self.table_in, self.own, send, recv = refs
        self.label_row = label_row
        self.images = self.table_out.shape[1]
        self.pieces = piece_ends
        count = len(piece_ends)
        self.is_end = owner * (3 - owner) == 0
        self.is_inner = owner * (3 - owner) != 0
        inner = 1 + lax.div(owner, 3)
        end = (owner - 1) * 3
        self.owner, self.end, self.far_inner, self.far_end = owner, end, 3 - owner, 3 - end

        def copy(at, source, target, device):
            return pltpu.make_async_remote_copy(
                src_ref=source,
                dst_ref=target,
                send_sem=send.at[at],
                recv_sem=recv.at[at],
                device_id={"dp": device},
                device_id_type=pl.DeviceIdType.MESH,
            )

        self.labels = copy(0, self.label_out, self.label_in, inner)
        self.copy = copy
        self.count = count
        self.inner = inner
        self.to_end = copy(1, self.table_out.at[0], self.table_in.at[0], end)

    def rows_copy(self, pair_v, k):
        first, size = self.pieces[k]
        part = (slice(None), pl.ds(first, size))
        return self.copy(2 + k, pair_v.at[part], self.pair_in.at[part], self.inner)

    def across_copy(self, slot, k):
        first, size = self.pieces[k]
        part = (slot, slice(None), pl.ds(first, size))
        device = self.far_inner if slot == 1 else self.far_end
        at = 2 + slot * self.count + k
        return self.copy(at, self.table_out.at[part], self.table_in.at[part], device)

    def onehot(self, label_row, device):
        rows = label_row.shape[1]
        ids = lax.broadcasted_iota(jnp.int32, (self.images, rows), 0) + device * self.images
        return jnp.where(ids.astype(jnp.float32) == label_row, 1.0, 0.0).astype(jnp.bfloat16)

    def tables(self, label_row, devices, values):
        hot = jnp.concatenate([self.onehot(label_row, d) for d in devices], axis=0)
        return jnp.dot(hot, values, preferred_element_type=jnp.float32)

    def send_labels(self):
        @pl.when(self.is_end)
        def _():
            self.labels.start()

    def first(self, pair_v, d_image_ref):
        images = self.images

        @pl.when(self.is_end)
        def _():
            for k in range(self.count):
                self.rows_copy(pair_v, k).start()
            d_image_ref[0] = self.tables(self.label_row, [self.owner], pair_v[...])

        @pl.when(self.is_inner)
        def _():
            self.table_out[0] = self.tables(self.label_row, [self.end], pair_v[...]).astype(jnp.bfloat16)
            self.to_end.start()
            devices = [self.far_inner, self.far_end, self.owner]
            self.own[...] = self.tables(self.label_row, devices, pair_v[...])
            self.labels.wait_recv()

    def step(self, pair_v, k, d_image_ref):
        first, size = self.pieces[k]
        images = self.images

        @pl.when(self.is_inner)
        def _():
            self.rows_copy(pair_v, k).wait_recv()
            part = pl.ds(first, size)
            devices = [self.far_inner, self.far_end, self.owner]
            there = self.label_in[pl.ds(0, 1)]
            sums = self.own[:, part] + self.tables(there, devices, self.pair_in[:, part])
            for slot in (1, 2):
                rows = sums[(slot - 1) * images : slot * images]
                self.table_out[slot, :, part] = rows.astype(jnp.bfloat16)
                self.across_copy(slot, k).start()
            d_image_ref[0, :, part] = sums[2 * images :]

    def last(self, pair_v, d_image_ref):
        @pl.when(self.is_end)
        def _():
            self.to_end.wait_recv()
            for k, (first, size) in enumerate(self.pieces):
                part = pl.ds(first, size)
                self.across_copy(2, k).wait_recv()
                d_image_ref[0, :, part] += (
                    self.table_in[0, :, part].astype(jnp.float32) + self.table_in[2, :, part].astype(jnp.float32)
                )
            self.labels.wait_send()
            for k in range(self.count):
                self.rows_copy(pair_v, k).wait_send()

        @pl.when(self.is_inner)
        def _():
            for k, (first, size) in enumerate(self.pieces):
                part = pl.ds(first, size)
                self.across_copy(1, k).wait_recv()
                d_image_ref[0, :, part] += self.table_in[1, :, part].astype(jnp.float32)
            self.to_end.wait_send()
            for k in range(self.count):
                self.across_copy(1, k).wait_send()
                self.across_copy(2, k).wait_send()


class Direct:
    def __init__(self, refs, owner, label_row, owners):
        self.table_out, self.table_in, self.send, self.recv = refs
        self.owner, self.label_row, self.owners = owner, label_row, owners

    def copy(self, apart):
        return pltpu.make_async_remote_copy(
            src_ref=self.table_out.at[apart],
            dst_ref=self.table_in.at[apart],
            send_sem=self.send.at[apart],
            recv_sem=self.recv.at[apart],
            device_id={"dp": lax.rem(self.owner + apart, self.owners)},
            device_id_type=pl.DeviceIdType.MESH,
        )

    def table(self, pair_v, apart):
        images, rows = self.table_out.shape[1], self.label_row.shape[1]
        first = lax.rem(self.owner + apart, self.owners) * images
        ids = lax.broadcasted_iota(jnp.int32, (images, rows), 0) + first
        onehot = jnp.where(ids.astype(jnp.float32) == self.label_row, 1.0, 0.0).astype(jnp.bfloat16)
        return jnp.dot(onehot, pair_v[...], preferred_element_type=jnp.float32)

    def send_labels(self):
        pass

    def first(self, pair_v, d_image_ref):
        for apart in range(1, self.owners):
            self.table_out[apart] = self.table(pair_v, apart).astype(jnp.bfloat16)
            self.copy(apart).start()
        d_image_ref[0] = self.table(pair_v, 0)

    def step(self, pair_v, k, d_image_ref):
        pass

    def last(self, pair_v, d_image_ref):
        for apart in range(1, self.owners):
            self.copy(apart).wait_recv()
            d_image_ref[0] += self.table_in[apart].astype(jnp.float32)
        for apart in range(1, self.owners):
            self.copy(apart).wait_send()


def pieces_of(width):
    lanes = width // 128
    small = max(lanes // 4, 1)
    sizes = [lanes - 3 * small] + [small] * 3 if lanes > 3 * small else [lanes]
    starts = [sum(sizes[:i]) for i in range(len(sizes))]
    return [(128 * a, 128 * b) for a, b in zip(starts, sizes)]


def kernel(
    owners,
    scale_ref,
    shift_ref,
    label_ref,
    image_ref,
    feat_ref,
    head_ref,
    d_feat_ref,
    d_image_ref,
    image_v,
    feat_v,
    head_v,
    xbuf,
    ybuf,
    unit_y_v,
    d_pair_v,
    load_sem,
    x_send,
    x_recv,
    y_send,
    y_recv,
    *dp_refs,
):
    rows, width = image_v.shape
    me = lax.axis_index("loop")
    owner = lax.axis_index("dp")

    load_image = pltpu.make_async_copy(image_ref.at[0], image_v, load_sem.at[0])
    load_feat = pltpu.make_async_copy(feat_ref.at[0], feat_v, load_sem.at[1])
    load_head = pltpu.make_async_copy(head_ref, head_v, load_sem.at[2])
    load_image.start()
    load_feat.start()
    load_head.start()

    barrier = pltpu.get_barrier_semaphore()
    for mask in (CORE, NEAR, FAR):
        pl.semaphore_signal(
            barrier, inc=1, device_id={"loop": partner(me, mask)}, device_id_type=pl.DeviceIdType.MESH
        )
    for apart in range(1, owners):
        pl.semaphore_signal(
            barrier,
            inc=1,
            device_id={"dp": lax.rem(owner + apart, owners)},
            device_id_type=pl.DeviceIdType.MESH,
        )

    scale = scale_ref[0]
    shift = shift_ref[0]
    label_row = label_ref[...].astype(jnp.float32)
    label_grid = jnp.broadcast_to(label_row, (rows, rows))
    same = label_grid == label_grid.T

    xs = Spread(xbuf, x_send, x_recv, me, rows)
    ys = Spread(ybuf, y_send, y_recv, me, rows)
    pieces = pieces_of(width)
    if owners == 4:
        sums = Line(dp_refs, owner, label_row, width, pieces)
        sums.label_out[...] = jnp.broadcast_to(label_row, sums.label_out.shape)
    else:
        sums = Direct(dp_refs, owner, label_row, owners)

    load_image.wait()
    image = image_v[...].astype(jnp.float32)
    inv_x = lax.rsqrt(jnp.sum(image * image, axis=-1, keepdims=True) + EPS)
    xbuf[pl.ds(0, rows)] = (image * inv_x).astype(jnp.bfloat16)

    pl.semaphore_wait(barrier, 3 + owners - 1)
    xs.near_a.start()
    xs.far_b.start()
    xs.own_core.start()
    sums.send_labels()

    load_feat.wait()
    load_head.wait()
    text_pre = jnp.dot(feat_v[...], head_v[...], preferred_element_type=jnp.float32)
    inv_y = lax.rsqrt(jnp.sum(text_pre * text_pre, axis=-1, keepdims=True) + EPS)
    unit_y = text_pre * inv_y
    ybuf[pl.ds(0, rows)] = unit_y.astype(jnp.bfloat16)
    ys.near_a.start()
    ys.far_b.start()
    ys.near_b.start()
    ys.far_a.start()
    ys.own_core.start()
    unit_y_v[...] = unit_y

    def part(mine, buf, slot, count):
        block = buf[pl.ds(slot * rows, count * rows)]
        logits = scale * lax.dot_general(mine, block, NT, preferred_element_type=jnp.float32) + shift
        if slot == 0:
            flip = jnp.concatenate([same, jnp.zeros_like(same)], axis=1)
            value = jax.nn.sigmoid(jnp.where(flip, -logits, logits))
            value = jnp.where(flip, -value, value)
        else:
            value = jax.nn.sigmoid(logits)
        return jnp.dot(value.astype(jnp.bfloat16), block, preferred_element_type=jnp.float32)

    x_own = xbuf[pl.ds(0, rows)]
    y_own = ybuf[pl.ds(0, rows)]

    ys.own_core.wait_recv()
    total = part(x_own, ybuf, 0, 2)
    ys.forward()
    ys.near_b.wait_recv()
    ys.near_core.start()
    ys.far_a.wait_recv()
    ys.far_core.start()
    ys.drain_diag()
    xs.near_b.start()
    xs.far_a.start()
    xs.forward()
    ys.near_core.wait_recv()
    total = total + part(x_own, ybuf, 2, 2)
    ys.far_core.wait_recv()
    total = total + part(x_own, ybuf, 4, 2)
    ys.relay_diag()
    total = total + part(x_own, ybuf, 6, 1)
    ys.await_diag_core()
    total = total + part(x_own, ybuf, 7, 1)
    grad = scale * total
    unit_x = image * inv_x
    d_pair = (grad - unit_x * jnp.sum(unit_x * grad, axis=-1, keepdims=True)) * inv_x
    d_pair_v[...] = d_pair.astype(jnp.bfloat16)

    sums.first(d_pair_v, d_image_ref)
    xs.near_b.wait_recv()
    xs.near_core.start()
    xs.far_a.wait_recv()
    xs.far_core.start()
    xs.own_core.wait_recv()
    total = part(y_own, xbuf, 0, 2)
    sums.step(d_pair_v, 0, d_image_ref)
    xs.near_core.wait_recv()
    total = total + part(y_own, xbuf, 2, 2)
    xs.far_core.wait_recv()
    total = total + part(y_own, xbuf, 4, 2)
    sums.step(d_pair_v, 1, d_image_ref)
    xs.relay_diag()
    total = total + part(y_own, xbuf, 6, 1)
    sums.step(d_pair_v, 2, d_image_ref)
    xs.await_diag_core()
    total = total + part(y_own, xbuf, 7, 1)
    sums.step(d_pair_v, 3, d_image_ref)
    grad = scale * total
    unit_y = unit_y_v[...]
    d_text = (grad - unit_y * jnp.sum(unit_y * grad, axis=-1, keepdims=True)) * inv_y
    d_feat_ref[0] = lax.dot_general(
        d_text.astype(jnp.bfloat16), head_v[...], NT, preferred_element_type=jnp.float32
    )

    sums.last(d_pair_v, d_image_ref)
    xs.drain(True)
    ys.drain(False)


def shards(owners, image_raw, text_feat, text_head, image_of_pair, logit_scale, logit_bias):
    _, rows, width = image_raw.shape
    depth = text_head.shape[0]
    images = rows // 2
    hbm = pl.BlockSpec(memory_space=pltpu.HBM)
    scalar = pl.BlockSpec(memory_space=pltpu.SMEM)
    vmem = pl.BlockSpec(memory_space=pltpu.VMEM)
    dma = pltpu.SemaphoreType.DMA
    if owners == 4:
        copies = 2 + 3 * len(pieces_of(width))
        dp_scratch = [
            pltpu.VMEM((8, rows), jnp.float32),
            pltpu.VMEM((8, rows), jnp.float32),
            pltpu.VMEM((rows, width), jnp.bfloat16),
            pltpu.VMEM((3, images, width), jnp.bfloat16),
            pltpu.VMEM((3, images, width), jnp.bfloat16),
            pltpu.VMEM((3 * images, width), jnp.float32),
            dma((copies,)),
            dma((copies,)),
        ]
    else:
        dp_scratch = [
            pltpu.VMEM((owners, images, width), jnp.bfloat16),
            pltpu.VMEM((owners, images, width), jnp.bfloat16),
            dma((owners,)),
            dma((owners,)),
        ]
    return pl.pallas_call(
        functools.partial(kernel, owners),
        out_shape=(
            jax.ShapeDtypeStruct((1, rows, depth), jnp.float32),
            jax.ShapeDtypeStruct((1, images, width), jnp.float32),
        ),
        in_specs=[scalar, scalar, vmem, hbm, hbm, hbm],
        out_specs=(vmem, vmem),
        scratch_shapes=[
            pltpu.VMEM((rows, width), jnp.bfloat16),
            pltpu.VMEM((rows, depth), jnp.bfloat16),
            pltpu.VMEM((depth, width), jnp.bfloat16),
            pltpu.VMEM((POOL_DEVS * rows, width), jnp.bfloat16),
            pltpu.VMEM((POOL_DEVS * rows, width), jnp.bfloat16),
            pltpu.VMEM((rows, width), jnp.float32),
            pltpu.VMEM((rows, width), jnp.bfloat16),
            dma((3,)),
            dma((COPIES,)),
            dma((COPIES,)),
            dma((COPIES,)),
            dma((COPIES,)),
            *dp_scratch,
        ],
        compiler_params=pltpu.CompilerParams(
            collective_id=0, has_side_effects=True, vmem_limit_bytes=56 * 1024 * 1024
        ),
    )(
        logit_scale.reshape((1,)),
        logit_bias.reshape((1,)),
        image_of_pair,
        image_raw,
        text_feat,
        text_head,
    )


def solution(mesh):
    placed = (P("dp", "loop", None), P("dp", "loop", None), P(), P("dp", "loop"), P(), P())
    return jax.shard_map(
        functools.partial(shards, mesh.shape["dp"]),
        mesh=mesh,
        in_specs=placed,
        out_specs=(P("dp", "loop", None), P("loop", "dp", None)),
        check_vma=False,
    )
```

```python
import functools

import jax
import jax.numpy as jnp
from jax import lax
from jax.experimental import pallas as pl
from jax.experimental.pallas import tpu as pltpu
from jax.sharding import PartitionSpec as P

EPS = 1e-06
CORE, NEAR, FAR = 1, 2, 4
NT = (((1,), (1,)), ((), ()))


def partner(me, mask):
    bit = lax.rem(lax.div(me, mask), 2)
    return me + mask * (1 - 2 * bit)


class Spread:
    def __init__(self, buf, send, recv, me, rows, mask):
        def copy(at, source, target, device, first, count):
            return pltpu.make_async_remote_copy(
                src_ref=buf.at[pl.ds(source * rows + first, count)],
                dst_ref=buf.at[pl.ds(target * rows + first, count)],
                send_sem=send.at[at],
                recv_sem=recv.at[at],
                device_id={"loop": device},
                device_id_type=pl.DeviceIdType.MESH,
            )

        core, side = partner(me, CORE), partner(me, mask)
        piece = rows // STEPS
        self.own_core = copy(0, 0, 2, core, 0, rows)
        self.direct = [copy(1 + i, 0, 1, side, i * piece, piece) for i in range(STEPS)]
        self.relay = [copy(1 + STEPS + i, 1, 3, core, i * piece, piece) for i in range(STEPS)]

    def start(self):
        for c in self.direct:
            c.start()
        self.own_core.start()

    def hand_on(self, i):
        self.direct[i].wait_recv()
        self.relay[i].start()

    def drain(self):
        for c in [self.own_core] + self.direct + self.relay:
            c.wait_send()


STEPS = 4
COPIES = 1 + 2 * STEPS


class Line:
    def __init__(self, refs, owner, label_row, pieces):
        self.label_out, self.label_in, self.pair_in, self.table_out, self.table_in, self.send, self.recv = refs
        self.label_row = label_row
        self.images = self.table_out.shape[1]
        self.pieces = pieces
        self.count = len(pieces)
        self.is_end = owner * (3 - owner) == 0
        self.is_inner = owner * (3 - owner) != 0
        self.inner = 1 + lax.div(owner, 3)
        self.end = (owner - 1) * 3
        self.owner, self.far_inner, self.far_end = owner, 3 - owner, 3 - self.end
        self.label_out[...] = jnp.broadcast_to(label_row, self.label_out.shape)
        self.labels = self.copy(0, self.label_out, self.label_in, self.inner)

    def copy(self, at, source, target, device):
        return pltpu.make_async_remote_copy(
            src_ref=source,
            dst_ref=target,
            send_sem=self.send.at[at],
            recv_sem=self.recv.at[at],
            device_id={"dp": device},
            device_id_type=pl.DeviceIdType.MESH,
        )

    def rows_copy(self, pair_v, k):
        part = (slice(None), pl.ds(*self.pieces[k]))
        return self.copy(1 + k, pair_v.at[part], self.pair_in.at[part], self.inner)

    def table_copy(self, slot, k):
        part = (slot, slice(None), pl.ds(*self.pieces[k]))
        device = (self.end, self.far_inner, self.far_end)[slot]
        at = 1 + (1 + slot) * self.count + k
        return self.copy(at, self.table_out.at[part], self.table_in.at[part], device)

    def tables(self, label_row, devices, values):
        rows = label_row.shape[1]
        ids = lax.broadcasted_iota(jnp.int32, (self.images, rows), 0).astype(jnp.float32)
        firsts = [(d * self.images).astype(jnp.float32) for d in devices]
        hot = jnp.concatenate([jnp.where(ids + f == label_row, 1.0, 0.0) for f in firsts], axis=0)
        return jnp.dot(hot.astype(jnp.bfloat16), values, preferred_element_type=jnp.float32)

    def send_labels(self):
        @pl.when(self.is_end)
        def _():
            self.labels.start()

    def ready(self, pair_v, k, d_image_ref):
        part = pl.ds(*self.pieces[k])

        @pl.when(self.is_end)
        def _():
            self.rows_copy(pair_v, k).start()
            d_image_ref[0, :, part] = self.tables(self.label_row, [self.owner], pair_v[:, part])

        @pl.when(self.is_inner)
        def _():
            self.table_out[0, :, part] = self.tables(self.label_row, [self.end], pair_v[:, part]).astype(jnp.bfloat16)
            self.table_copy(0, k).start()
            if k == 0:
                self.labels.wait_recv()

    def step(self, pair_v, k, d_image_ref):
        images = self.images
        part = pl.ds(*self.pieces[k])

        @pl.when(self.is_inner)
        def _():
            devices = [self.far_inner, self.far_end, self.owner]
            sums = self.tables(self.label_row, devices, pair_v[:, part])
            self.rows_copy(pair_v, k).wait_recv()
            sums = sums + self.tables(self.label_in[pl.ds(0, 1)], devices, self.pair_in[:, part])
            for slot in (1, 2):
                self.table_out[slot, :, part] = sums[(slot - 1) * images : slot * images].astype(jnp.bfloat16)
                self.table_copy(slot, k).start()
            d_image_ref[0, :, part] = sums[2 * images :]

    def last(self, pair_v, d_image_ref):
        @pl.when(self.is_end)
        def _():
            for k, piece in enumerate(self.pieces):
                part = pl.ds(*piece)
                self.table_copy(0, k).wait_recv()
                self.table_copy(2, k).wait_recv()
                d_image_ref[0, :, part] += (
                    self.table_in[0, :, part].astype(jnp.float32) + self.table_in[2, :, part].astype(jnp.float32)
                )
            self.labels.wait_send()
            for k in range(self.count):
                self.rows_copy(pair_v, k).wait_send()

        @pl.when(self.is_inner)
        def _():
            for k, piece in enumerate(self.pieces):
                part = pl.ds(*piece)
                self.table_copy(1, k).wait_recv()
                d_image_ref[0, :, part] += self.table_in[1, :, part].astype(jnp.float32)
            for k in range(self.count):
                for slot in range(3):
                    self.table_copy(slot, k).wait_send()


class Direct:
    def __init__(self, refs, owner, label_row, owners):
        self.table_out, self.table_in, self.send, self.recv = refs
        self.owner, self.label_row, self.owners = owner, label_row, owners

    def copy(self, apart):
        return pltpu.make_async_remote_copy(
            src_ref=self.table_out.at[apart],
            dst_ref=self.table_in.at[apart],
            send_sem=self.send.at[apart],
            recv_sem=self.recv.at[apart],
            device_id={"dp": lax.rem(self.owner + apart, self.owners)},
            device_id_type=pl.DeviceIdType.MESH,
        )

    def table(self, pair_v, apart):
        images, rows = self.table_out.shape[1], self.label_row.shape[1]
        first = lax.rem(self.owner + apart, self.owners) * images
        ids = lax.broadcasted_iota(jnp.int32, (images, rows), 0) + first
        onehot = jnp.where(ids.astype(jnp.float32) == self.label_row, 1.0, 0.0).astype(jnp.bfloat16)
        return jnp.dot(onehot, pair_v[...], preferred_element_type=jnp.float32)

    def send_labels(self):
        pass

    def ready(self, pair_v, k, d_image_ref):
        if k + 1 < len(pieces_of(pair_v.shape[1])):
            return
        for apart in range(1, self.owners):
            self.table_out[apart] = self.table(pair_v, apart).astype(jnp.bfloat16)
            self.copy(apart).start()
        d_image_ref[0] = self.table(pair_v, 0)

    def step(self, pair_v, k, d_image_ref):
        pass

    def last(self, pair_v, d_image_ref):
        for apart in range(1, self.owners):
            self.copy(apart).wait_recv()
            d_image_ref[0] += self.table_in[apart].astype(jnp.float32)
        for apart in range(1, self.owners):
            self.copy(apart).wait_send()


def pieces_of(width):
    lanes = width // 128
    small = max(lanes // 4, 1)
    sizes = [lanes - 3 * small] + [small] * 3 if lanes > 3 * small else [lanes]
    starts = [sum(sizes[:i]) for i in range(len(sizes))]
    return [(128 * a, 128 * b) for a, b in zip(starts, sizes)]


def kernel(
    owners,
    scale_ref,
    shift_ref,
    label_ref,
    image_ref,
    feat_ref,
    head_ref,
    d_feat_ref,
    d_image_ref,
    label_v,
    image_v,
    feat_v,
    head_v,
    xbuf,
    ybuf,
    x_weight,
    y_weight,
    unit_y_v,
    text_v,
    d_pair_v,
    x_out,
    x_in,
    y_out,
    y_in,
    dots_out,
    dots_in,
    load_sem,
    x_send,
    x_recv,
    y_send,
    y_recv,
    px_send,
    px_recv,
    py_send,
    py_recv,
    *dp_refs,
):
    rows, width = image_v.shape
    me = lax.axis_index("loop")
    owner = lax.axis_index("dp")

    load_image = pltpu.make_async_copy(image_ref.at[0], image_v, load_sem.at[0])
    load_feat = pltpu.make_async_copy(feat_ref.at[0], feat_v, load_sem.at[1])
    load_head = pltpu.make_async_copy(head_ref, head_v, load_sem.at[2])
    load_label = pltpu.make_async_copy(label_ref, label_v, load_sem.at[3])
    load_label.start()
    load_image.start()
    load_feat.start()
    load_head.start()

    barrier = pltpu.get_barrier_semaphore()
    for mask in (CORE, NEAR, FAR):
        pl.semaphore_signal(
            barrier, inc=1, device_id={"loop": partner(me, mask)}, device_id_type=pl.DeviceIdType.MESH
        )
    for apart in range(1, owners):
        pl.semaphore_signal(
            barrier,
            inc=1,
            device_id={"dp": lax.rem(owner + apart, owners)},
            device_id_type=pl.DeviceIdType.MESH,
        )

    scale = scale_ref[0]
    shift = shift_ref[0]
    load_label.wait()
    label_row = label_v[...].astype(jnp.float32)
    label_grid = jnp.broadcast_to(label_row, (rows, rows))
    same = label_grid == label_grid.T

    xs = Spread(xbuf, x_send, x_recv, me, rows, NEAR)
    ys = Spread(ybuf, y_send, y_recv, me, rows, FAR)
    pieces = pieces_of(width)
    if owners == 4:
        sums = Line(dp_refs, owner, label_row, pieces)
    else:
        sums = Direct(dp_refs, owner, label_row, owners)

    def side_copy(source, target, send, recv, at, mask):
        return pltpu.make_async_remote_copy(
            src_ref=source,
            dst_ref=target,
            send_sem=send.at[at],
            recv_sem=recv.at[at],
            device_id={"loop": partner(me, mask)},
            device_id_type=pl.DeviceIdType.MESH,
        )

    columns = [(slice(None), pl.ds(*piece)) for piece in pieces]
    x_parts = [side_copy(x_out.at[c], x_in.at[c], px_send, px_recv, k, NEAR) for k, c in enumerate(columns)]
    y_parts = [side_copy(y_out.at[c], y_in.at[c], py_send, py_recv, k, FAR) for k, c in enumerate(columns)]
    dots_copy = side_copy(dots_out, dots_in, px_send, px_recv, len(pieces), NEAR)

    load_image.wait()
    image = image_v[...].astype(jnp.float32)
    inv_x = lax.rsqrt(jnp.sum(image * image, axis=-1, keepdims=True) + EPS)
    xbuf[pl.ds(0, rows)] = (image * inv_x).astype(jnp.bfloat16)

    pl.semaphore_wait(barrier, 3 + owners - 1)
    xs.start()
    sums.send_labels()

    load_feat.wait()
    load_head.wait()
    text_pre = jnp.dot(feat_v[...], head_v[...], preferred_element_type=jnp.float32)
    inv_y = lax.rsqrt(jnp.sum(text_pre * text_pre, axis=-1, keepdims=True) + EPS)
    unit_y = text_pre * inv_y
    ybuf[pl.ds(0, rows)] = unit_y.astype(jnp.bfloat16)
    ys.start()
    unit_y_v[...] = unit_y

    def weights(mine, first, count, other, block, blocks, weight):
        dots = lax.dot_general(
            mine[pl.ds(first * rows, count * rows)],
            other[pl.ds(block * rows, blocks * rows)],
            NT,
            preferred_element_type=jnp.float32,
        )
        logits = scale * dots + shift
        if first == 0 and block == 0:
            value = jax.nn.sigmoid(jnp.where(same, -logits, logits))
            value = jnp.where(same, -value, value)
        else:
            value = jax.nn.sigmoid(logits)
        value = value.astype(jnp.bfloat16)
        weight[pl.ds(first * rows, count * rows), pl.ds(block * rows, blocks * rows)] = value
        return jnp.sum(value.astype(jnp.float32) * dots, axis=-1, keepdims=True)

    def product(weight, first, buf, column):
        return jnp.dot(weight[pl.ds(first * rows, rows)], buf[column], preferred_element_type=jnp.float32)

    xs.hand_on(0)
    ys.own_core.wait_recv()
    xs.own_core.wait_recv()
    own_dots = weights(xbuf, 0, 1, ybuf, 0, 1, x_weight) + weights(xbuf, 0, 1, ybuf, 2, 1, x_weight)
    weights(ybuf, 0, 1, xbuf, 0, 1, y_weight)
    weights(ybuf, 0, 1, xbuf, 2, 1, y_weight)
    xs.hand_on(1)
    ys.hand_on(0)
    xs.hand_on(2)
    ys.hand_on(1)
    xs.hand_on(3)
    ys.hand_on(2)
    near_dots = weights(xbuf, 1, 1, ybuf, 0, 1, x_weight) + weights(xbuf, 1, 1, ybuf, 2, 1, x_weight)
    ys.hand_on(3)

    near_dots = near_dots + weights(xbuf, 1, 1, ybuf, 1, 1, x_weight)
    for c in ys.relay:
        c.wait_recv()
    near_dots = near_dots + weights(xbuf, 1, 1, ybuf, 3, 1, x_weight)
    dots_out[...] = jnp.broadcast_to(near_dots, (rows, rows)).T[:8]
    dots_copy.start()
    for k, c in enumerate(columns):
        x_out[c] = product(x_weight, 1, ybuf, c).astype(jnp.bfloat16)
        x_parts[k].start()

    for c in xs.relay:
        c.wait_recv()
    weights(ybuf, 1, 1, xbuf, 0, 4, y_weight)
    for k, c in enumerate(columns):
        y_out[c] = product(y_weight, 1, xbuf, c).astype(jnp.bfloat16)
        y_parts[k].start()

    own_dots = own_dots + weights(xbuf, 0, 1, ybuf, 1, 1, x_weight) + weights(xbuf, 0, 1, ybuf, 3, 1, x_weight)
    weights(ybuf, 0, 1, xbuf, 1, 1, y_weight)
    weights(ybuf, 0, 1, xbuf, 3, 1, y_weight)
    for c in columns:
        text_v[c] = product(y_weight, 0, xbuf, c)
    dots_copy.wait_recv()
    there = jnp.broadcast_to(dots_in[pl.ds(0, 1)], (rows, rows)).T[:, :1]
    along = scale * (own_dots + there)
    for k, c in enumerate(columns):
        grad = product(x_weight, 0, ybuf, c)
        unit_x = image_v[c].astype(jnp.float32) * inv_x
        x_parts[k].wait_recv()
        grad = scale * (grad + x_in[c].astype(jnp.float32))
        d_pair_v[c] = ((grad - unit_x * along) * inv_x).astype(jnp.bfloat16)
        sums.ready(d_pair_v, k, d_image_ref)
        if k > 0:
            sums.step(d_pair_v, k - 1, d_image_ref)

    for c in y_parts:
        c.wait_recv()
    grad = scale * (text_v[...] + y_in[...].astype(jnp.float32))
    unit_y = unit_y_v[...]
    d_text = (grad - unit_y * jnp.sum(unit_y * grad, axis=-1, keepdims=True)) * inv_y
    sums.step(d_pair_v, len(pieces) - 1, d_image_ref)
    d_feat_ref[0] = lax.dot_general(
        d_text.astype(jnp.bfloat16), head_v[...], NT, preferred_element_type=jnp.float32
    )

    sums.last(d_pair_v, d_image_ref)
    xs.drain()
    ys.drain()
    for c in x_parts + y_parts + [dots_copy]:
        c.wait_send()


def store(feat_v, image_v, d_feat_ref, d_image_ref, sem):
    feat = pltpu.make_async_copy(feat_v, d_feat_ref, sem.at[0])
    image = pltpu.make_async_copy(image_v, d_image_ref, sem.at[1])
    feat.start()
    image.start()
    feat.wait()
    image.wait()


def shards(owners, image_raw, text_feat, text_head, image_of_pair, logit_scale, logit_bias):
    _, rows, width = image_raw.shape
    depth = text_head.shape[0]
    images = rows // 2
    hbm = pl.BlockSpec(memory_space=pltpu.HBM)
    scalar = pl.BlockSpec(memory_space=pltpu.SMEM)
    vmem = pl.BlockSpec(memory_space=pltpu.VMEM)
    dma = pltpu.SemaphoreType.DMA
    count = len(pieces_of(width))
    if owners == 4:
        dp_scratch = [
            pltpu.VMEM((8, rows), jnp.float32),
            pltpu.VMEM((8, rows), jnp.float32),
            pltpu.VMEM((rows, width), jnp.bfloat16),
            pltpu.VMEM((3, images, width), jnp.bfloat16),
            pltpu.VMEM((3, images, width), jnp.bfloat16),
            dma((1 + 4 * count,)),
            dma((1 + 4 * count,)),
        ]
    else:
        dp_scratch = [
            pltpu.VMEM((owners, images, width), jnp.bfloat16),
            pltpu.VMEM((owners, images, width), jnp.bfloat16),
            dma((owners,)),
            dma((owners,)),
        ]
    results = (
        jax.ShapeDtypeStruct((1, rows, depth), jnp.float32),
        jax.ShapeDtypeStruct((1, images, width), jnp.float32),
    )
    gradients = pl.pallas_call(
        functools.partial(kernel, owners),
        out_shape=results,
        in_specs=[scalar, scalar, hbm, hbm, hbm, hbm],
        out_specs=(vmem, vmem),
        scratch_shapes=[
            pltpu.VMEM((1, rows), jnp.int32),
            pltpu.VMEM((rows, width), jnp.bfloat16),
            pltpu.VMEM((rows, depth), jnp.bfloat16),
            pltpu.VMEM((depth, width), jnp.bfloat16),
            pltpu.VMEM((4 * rows, width), jnp.bfloat16),
            pltpu.VMEM((4 * rows, width), jnp.bfloat16),
            pltpu.VMEM((2 * rows, 4 * rows), jnp.bfloat16),
            pltpu.VMEM((2 * rows, 4 * rows), jnp.bfloat16),
            pltpu.VMEM((rows, width), jnp.float32),
            pltpu.VMEM((rows, width), jnp.float32),
            pltpu.VMEM((rows, width), jnp.bfloat16),
            pltpu.VMEM((rows, width), jnp.bfloat16),
            pltpu.VMEM((rows, width), jnp.bfloat16),
            pltpu.VMEM((rows, width), jnp.bfloat16),
            pltpu.VMEM((rows, width), jnp.bfloat16),
            pltpu.VMEM((8, rows), jnp.float32),
            pltpu.VMEM((8, rows), jnp.float32),
            dma((4,)),
            dma((COPIES,)),
            dma((COPIES,)),
            dma((COPIES,)),
            dma((COPIES,)),
            dma((count + 1,)),
            dma((count + 1,)),
            dma((count,)),
            dma((count,)),
            *dp_scratch,
        ],
        compiler_params=pltpu.CompilerParams(
            collective_id=0, has_side_effects=True, vmem_limit_bytes=32 * 1024 * 1024
        ),
    )(
        logit_scale.reshape((1,)),
        logit_bias.reshape((1,)),
        *(
            pltpu.with_memory_space_constraint(a, pltpu.HBM)
            for a in (image_of_pair, image_raw, text_feat, text_head)
        ),
    )
    return pl.pallas_call(
        store,
        out_shape=results,
        in_specs=[vmem, vmem],
        out_specs=(hbm, hbm),
        scratch_shapes=[dma((2,))],
    )(*gradients)


def solution(mesh):
    placed = (P("dp", "loop", None), P("dp", "loop", None), P(), P("dp", "loop"), P(), P())
    return jax.shard_map(
        functools.partial(shards, mesh.shape["dp"]),
        mesh=mesh,
        in_specs=placed,
        out_specs=(P("dp", "loop", None), P("loop", "dp", None)),
        check_vma=False,
    )
```

```python
import functools

import jax
import jax.numpy as jnp
from jax import lax
from jax.experimental import pallas as pl
from jax.experimental.pallas import tpu as pltpu
from jax.sharding import PartitionSpec as P

EPS = 1e-06
CORE, NEAR, FAR = 1, 2, 4
NT = (((1,), (1,)), ((), ()))


def partner(me, mask):
    bit = lax.rem(lax.div(me, mask), 2)
    return me + mask * (1 - 2 * bit)


class Spread:
    def __init__(self, buf, send, recv, me, rows, mask):
        def copy(at, source, target, device, first, count):
            return pltpu.make_async_remote_copy(
                src_ref=buf.at[pl.ds(source * rows + first, count)],
                dst_ref=buf.at[pl.ds(target * rows + first, count)],
                send_sem=send.at[at],
                recv_sem=recv.at[at],
                device_id={"loop": device},
                device_id_type=pl.DeviceIdType.MESH,
            )

        core, side = partner(me, CORE), partner(me, mask)
        piece = rows // STEPS
        self.own_core = copy(0, 0, 2, core, 0, rows)
        self.direct = [copy(1 + i, 0, 1, side, i * piece, piece) for i in range(STEPS)]
        self.relay = [copy(1 + STEPS + i, 1, 3, core, i * piece, piece) for i in range(STEPS)]

    def start(self):
        for c in self.direct:
            c.start()
        self.own_core.start()

    def hand_on(self, i):
        self.direct[i].wait_recv()
        self.relay[i].start()

    def drain(self):
        for c in [self.own_core] + self.direct + self.relay:
            c.wait_send()


STEPS = 4
COPIES = 1 + 2 * STEPS
LAG = 3


class Line:
    def __init__(self, refs, owner, label_row, pieces):
        self.label_out, self.label_in, self.pair_in, self.table_out, self.table_in, self.hot, self.send, self.recv = refs
        self.label_row = label_row
        self.images = self.table_out.shape[1]
        self.pieces = pieces
        self.count = len(pieces)
        self.is_end = owner * (3 - owner) == 0
        self.is_inner = owner * (3 - owner) != 0
        self.inner = 1 + lax.div(owner, 3)
        self.end = (owner - 1) * 3
        self.owner, self.far_inner, self.far_end = owner, 3 - owner, 3 - self.end
        self.label_out[...] = jnp.broadcast_to(label_row, self.label_out.shape)
        self.labels = self.copy(0, self.label_out, self.label_in, self.inner)

    def copy(self, at, source, target, device):
        return pltpu.make_async_remote_copy(
            src_ref=source,
            dst_ref=target,
            send_sem=self.send.at[at],
            recv_sem=self.recv.at[at],
            device_id={"dp": device},
            device_id_type=pl.DeviceIdType.MESH,
        )

    def rows_copy(self, pair_v, k):
        part = (slice(None), pl.ds(*self.pieces[k]))
        return self.copy(1 + k, pair_v.at[part], self.pair_in.at[part], self.inner)

    def table_copy(self, slot, k):
        part = (slot, slice(None), pl.ds(*self.pieces[k]))
        device = (self.end, self.far_inner, self.far_end)[slot]
        at = 1 + (1 + slot) * self.count + k
        return self.copy(at, self.table_out.at[part], self.table_in.at[part], device)

    def mark(self, at, label_row, devices):
        images, rows = self.images, label_row.shape[1]
        ids = lax.broadcasted_iota(jnp.int32, (images, rows), 0).astype(jnp.float32)
        for i, device in enumerate(devices):
            hot = jnp.where(ids + (device * images).astype(jnp.float32) == label_row, 1.0, 0.0)
            self.hot[pl.ds((at + i) * images, images)] = hot.astype(jnp.bfloat16)

    def tables(self, at, count, values):
        hot = self.hot[pl.ds(at * self.images, count * self.images)]
        return jnp.dot(hot, values, preferred_element_type=jnp.float32)

    def prepare(self):
        @pl.when(self.is_end)
        def _():
            self.mark(0, self.label_row, [self.owner])

        @pl.when(self.is_inner)
        def _():
            devices = [self.far_inner, self.far_end, self.owner]
            self.mark(0, self.label_row, [self.end] + devices)
            self.labels.wait_recv()
            self.mark(4, self.label_in[pl.ds(0, 1)], devices)

    def send_labels(self):
        @pl.when(self.is_end)
        def _():
            self.labels.start()

    def ready(self, pair_v, k, d_image_ref):
        part = pl.ds(*self.pieces[k])

        @pl.when(self.is_end)
        def _():
            self.rows_copy(pair_v, k).start()
            d_image_ref[0, :, part] = self.tables(0, 1, pair_v[:, part])

        @pl.when(self.is_inner)
        def _():
            self.table_out[0, :, part] = self.tables(0, 1, pair_v[:, part]).astype(jnp.bfloat16)
            self.table_copy(0, k).start()

    def step(self, pair_v, k, d_image_ref):
        images = self.images
        part = pl.ds(*self.pieces[k])

        @pl.when(self.is_inner)
        def _():
            sums = self.tables(1, 3, pair_v[:, part])
            self.rows_copy(pair_v, k).wait_recv()
            sums = sums + self.tables(4, 3, self.pair_in[:, part])
            for slot in (1, 2):
                self.table_out[slot, :, part] = sums[(slot - 1) * images : slot * images].astype(jnp.bfloat16)
                self.table_copy(slot, k).start()
            d_image_ref[0, :, part] = sums[2 * images :]

    def last(self, pair_v, d_image_ref):
        @pl.when(self.is_end)
        def _():
            for k, piece in enumerate(self.pieces):
                part = pl.ds(*piece)
                self.table_copy(0, k).wait_recv()
                self.table_copy(2, k).wait_recv()
                d_image_ref[0, :, part] += (
                    self.table_in[0, :, part].astype(jnp.float32) + self.table_in[2, :, part].astype(jnp.float32)
                )
            self.labels.wait_send()
            for k in range(self.count):
                self.rows_copy(pair_v, k).wait_send()

        @pl.when(self.is_inner)
        def _():
            for k, piece in enumerate(self.pieces):
                part = pl.ds(*piece)
                self.table_copy(1, k).wait_recv()
                d_image_ref[0, :, part] += self.table_in[1, :, part].astype(jnp.float32)
            for k in range(self.count):
                for slot in range(3):
                    self.table_copy(slot, k).wait_send()


class Direct:
    def __init__(self, refs, owner, label_row, owners):
        self.table_out, self.table_in, self.send, self.recv = refs
        self.owner, self.label_row, self.owners = owner, label_row, owners

    def copy(self, apart):
        return pltpu.make_async_remote_copy(
            src_ref=self.table_out.at[apart],
            dst_ref=self.table_in.at[apart],
            send_sem=self.send.at[apart],
            recv_sem=self.recv.at[apart],
            device_id={"dp": lax.rem(self.owner + apart, self.owners)},
            device_id_type=pl.DeviceIdType.MESH,
        )

    def table(self, pair_v, apart):
        images, rows = self.table_out.shape[1], self.label_row.shape[1]
        first = lax.rem(self.owner + apart, self.owners) * images
        ids = lax.broadcasted_iota(jnp.int32, (images, rows), 0) + first
        onehot = jnp.where(ids.astype(jnp.float32) == self.label_row, 1.0, 0.0).astype(jnp.bfloat16)
        return jnp.dot(onehot, pair_v[...], preferred_element_type=jnp.float32)

    def send_labels(self):
        pass

    def prepare(self):
        pass

    def ready(self, pair_v, k, d_image_ref):
        if k + 1 < len(pieces_of(pair_v.shape[1])):
            return
        for apart in range(1, self.owners):
            self.table_out[apart] = self.table(pair_v, apart).astype(jnp.bfloat16)
            self.copy(apart).start()
        d_image_ref[0] = self.table(pair_v, 0)

    def step(self, pair_v, k, d_image_ref):
        pass

    def last(self, pair_v, d_image_ref):
        for apart in range(1, self.owners):
            self.copy(apart).wait_recv()
            d_image_ref[0] += self.table_in[apart].astype(jnp.float32)
        for apart in range(1, self.owners):
            self.copy(apart).wait_send()


def pieces_of(width):
    return [(first, 128) for first in range(0, width, 128)]


def kernel(
    owners,
    scale_ref,
    shift_ref,
    label_ref,
    image_ref,
    feat_ref,
    head_ref,
    d_feat_ref,
    d_image_ref,
    label_v,
    image_v,
    feat_v,
    head_v,
    xbuf,
    ybuf,
    x_weight,
    y_weight,
    unit_y_v,
    text_v,
    d_pair_v,
    x_out,
    x_in,
    y_out,
    y_in,
    dots_out,
    dots_in,
    load_sem,
    x_send,
    x_recv,
    y_send,
    y_recv,
    px_send,
    px_recv,
    py_send,
    py_recv,
    *dp_refs,
):
    rows, width = image_v.shape
    me = lax.axis_index("loop")
    owner = lax.axis_index("dp")

    barrier = pltpu.get_barrier_semaphore()
    for mask in (CORE, NEAR, FAR):
        pl.semaphore_signal(
            barrier, inc=1, device_id={"loop": partner(me, mask)}, device_id_type=pl.DeviceIdType.MESH
        )
    for apart in range(1, owners):
        pl.semaphore_signal(
            barrier,
            inc=1,
            device_id={"dp": lax.rem(owner + apart, owners)},
            device_id_type=pl.DeviceIdType.MESH,
        )

    load_image = pltpu.make_async_copy(image_ref.at[0], image_v, load_sem.at[0])
    load_feat = pltpu.make_async_copy(feat_ref.at[0], feat_v, load_sem.at[1])
    load_head = pltpu.make_async_copy(head_ref, head_v, load_sem.at[2])
    load_label = pltpu.make_async_copy(label_ref, label_v, load_sem.at[3])
    load_label.start()
    load_image.start()
    load_feat.start()
    load_head.start()

    scale = scale_ref[0]
    shift = shift_ref[0]
    load_label.wait()
    label_row = label_v[...].astype(jnp.float32)
    label_grid = jnp.broadcast_to(label_row, (rows, rows))
    same = label_grid == label_grid.T

    xs = Spread(xbuf, x_send, x_recv, me, rows, NEAR)
    ys = Spread(ybuf, y_send, y_recv, me, rows, FAR)
    pieces = pieces_of(width)
    if owners == 4:
        sums = Line(dp_refs, owner, label_row, pieces)
    else:
        sums = Direct(dp_refs, owner, label_row, owners)

    def side_copy(source, target, send, recv, at, mask):
        return pltpu.make_async_remote_copy(
            src_ref=source,
            dst_ref=target,
            send_sem=send.at[at],
            recv_sem=recv.at[at],
            device_id={"loop": partner(me, mask)},
            device_id_type=pl.DeviceIdType.MESH,
        )

    columns = [(slice(None), pl.ds(*piece)) for piece in pieces]
    x_parts = [side_copy(x_out.at[c], x_in.at[c], px_send, px_recv, k, NEAR) for k, c in enumerate(columns)]
    y_parts = [side_copy(y_out.at[c], y_in.at[c], py_send, py_recv, k, FAR) for k, c in enumerate(columns)]
    dots_copy = side_copy(dots_out, dots_in, px_send, px_recv, len(pieces), NEAR)

    load_image.wait()
    image = image_v[...].astype(jnp.float32)
    inv_x = lax.rsqrt(jnp.sum(image * image, axis=-1, keepdims=True) + EPS)
    xbuf[pl.ds(0, rows)] = (image * inv_x).astype(jnp.bfloat16)

    load_feat.wait()
    load_head.wait()
    text_pre = jnp.dot(feat_v[...], head_v[...], preferred_element_type=jnp.float32)
    inv_y = lax.rsqrt(jnp.sum(text_pre * text_pre, axis=-1, keepdims=True) + EPS)
    unit_y = text_pre * inv_y
    ybuf[pl.ds(0, rows)] = unit_y.astype(jnp.bfloat16)
    pl.semaphore_wait(barrier, 3 + owners - 1)
    ys.start()
    xs.start()
    sums.send_labels()
    unit_y_v[...] = unit_y

    def weights(mine, first, count, other, block, blocks, weight):
        dots = lax.dot_general(
            mine[pl.ds(first * rows, count * rows)],
            other[pl.ds(block * rows, blocks * rows)],
            NT,
            preferred_element_type=jnp.float32,
        )
        logits = scale * dots + shift
        if first == 0 and block == 0:
            value = jax.nn.sigmoid(jnp.where(same, -logits, logits))
            value = jnp.where(same, -value, value)
        else:
            value = jax.nn.sigmoid(logits)
        value = value.astype(jnp.bfloat16)
        weight[pl.ds(first * rows, count * rows), pl.ds(block * rows, blocks * rows)] = value
        return jnp.sum(value.astype(jnp.float32) * dots, axis=-1, keepdims=True)

    def product(weight, first, buf, column):
        return jnp.dot(weight[pl.ds(first * rows, rows)], buf[column], preferred_element_type=jnp.float32)

    xs.hand_on(0)
    ys.own_core.wait_recv()
    xs.own_core.wait_recv()
    own_dots = weights(xbuf, 0, 1, ybuf, 0, 1, x_weight) + weights(xbuf, 0, 1, ybuf, 2, 1, x_weight)
    weights(ybuf, 0, 1, xbuf, 0, 1, y_weight)
    weights(ybuf, 0, 1, xbuf, 2, 1, y_weight)
    xs.hand_on(1)
    ys.hand_on(0)
    xs.hand_on(2)
    ys.hand_on(1)
    xs.hand_on(3)
    ys.hand_on(2)
    near_dots = weights(xbuf, 1, 1, ybuf, 0, 1, x_weight) + weights(xbuf, 1, 1, ybuf, 2, 1, x_weight)
    ys.hand_on(3)

    near_dots = near_dots + weights(xbuf, 1, 1, ybuf, 1, 1, x_weight)
    for c in ys.relay:
        c.wait_recv()
    near_dots = near_dots + weights(xbuf, 1, 1, ybuf, 3, 1, x_weight)
    dots_out[...] = jnp.broadcast_to(near_dots, (rows, rows)).T[:8]
    dots_copy.start()
    for k, c in enumerate(columns):
        x_out[c] = product(x_weight, 1, ybuf, c).astype(jnp.bfloat16)
        x_parts[k].start()

    for c in xs.relay:
        c.wait_recv()
    weights(ybuf, 1, 1, xbuf, 0, 4, y_weight)
    for k, c in enumerate(columns):
        y_out[c] = product(y_weight, 1, xbuf, c).astype(jnp.bfloat16)
        y_parts[k].start()

    own_dots = own_dots + weights(xbuf, 0, 1, ybuf, 1, 1, x_weight) + weights(xbuf, 0, 1, ybuf, 3, 1, x_weight)
    weights(ybuf, 0, 1, xbuf, 1, 1, y_weight)
    weights(ybuf, 0, 1, xbuf, 3, 1, y_weight)
    for c in columns:
        text_v[c] = product(y_weight, 0, xbuf, c)
    sums.prepare()
    dots_copy.wait_recv()
    there = jnp.broadcast_to(dots_in[pl.ds(0, 1)], (rows, rows)).T[:, :1]
    along = scale * (own_dots + there)
    for k, c in enumerate(columns):
        grad = product(x_weight, 0, ybuf, c)
        unit_x = image_v[c].astype(jnp.float32) * inv_x
        x_parts[k].wait_recv()
        grad = scale * (grad + x_in[c].astype(jnp.float32))
        d_pair_v[c] = ((grad - unit_x * along) * inv_x).astype(jnp.bfloat16)
        sums.ready(d_pair_v, k, d_image_ref)
        if k >= LAG:
            sums.step(d_pair_v, k - LAG, d_image_ref)

    for k in range(len(pieces) - LAG, len(pieces) - 1):
        sums.step(d_pair_v, k, d_image_ref)
    for c in y_parts:
        c.wait_recv()
    grad = scale * (text_v[...] + y_in[...].astype(jnp.float32))
    unit_y = unit_y_v[...]
    d_text = (grad - unit_y * jnp.sum(unit_y * grad, axis=-1, keepdims=True)) * inv_y
    sums.step(d_pair_v, len(pieces) - 1, d_image_ref)
    d_feat_ref[0] = lax.dot_general(
        d_text.astype(jnp.bfloat16), head_v[...], NT, preferred_element_type=jnp.float32
    )

    sums.last(d_pair_v, d_image_ref)
    xs.drain()
    ys.drain()
    for c in x_parts + y_parts + [dots_copy]:
        c.wait_send()


def store(feat_v, image_v, d_feat_ref, d_image_ref, sem):
    feat = pltpu.make_async_copy(feat_v, d_feat_ref, sem.at[0])
    image = pltpu.make_async_copy(image_v, d_image_ref, sem.at[1])
    feat.start()
    image.start()
    feat.wait()
    image.wait()


def shards(owners, image_raw, text_feat, text_head, image_of_pair, logit_scale, logit_bias):
    _, rows, width = image_raw.shape
    depth = text_head.shape[0]
    images = rows // 2
    hbm = pl.BlockSpec(memory_space=pltpu.HBM)
    scalar = pl.BlockSpec(memory_space=pltpu.SMEM)
    vmem = pl.BlockSpec(memory_space=pltpu.VMEM)
    dma = pltpu.SemaphoreType.DMA
    count = len(pieces_of(width))
    if owners == 4:
        dp_scratch = [
            pltpu.VMEM((8, rows), jnp.float32),
            pltpu.VMEM((8, rows), jnp.float32),
            pltpu.VMEM((rows, width), jnp.bfloat16),
            pltpu.VMEM((3, images, width), jnp.bfloat16),
            pltpu.VMEM((3, images, width), jnp.bfloat16),
            pltpu.VMEM((7 * images, rows), jnp.bfloat16),
            dma((1 + 4 * count,)),
            dma((1 + 4 * count,)),
        ]
    else:
        dp_scratch = [
            pltpu.VMEM((owners, images, width), jnp.bfloat16),
            pltpu.VMEM((owners, images, width), jnp.bfloat16),
            dma((owners,)),
            dma((owners,)),
        ]
    results = (
        jax.ShapeDtypeStruct((1, rows, depth), jnp.float32),
        jax.ShapeDtypeStruct((1, images, width), jnp.float32),
    )
    gradients = pl.pallas_call(
        functools.partial(kernel, owners),
        out_shape=results,
        in_specs=[scalar, scalar, hbm, hbm, hbm, hbm],
        out_specs=(vmem, vmem),
        scratch_shapes=[
            pltpu.VMEM((1, rows), jnp.int32),
            pltpu.VMEM((rows, width), jnp.bfloat16),
            pltpu.VMEM((rows, depth), jnp.bfloat16),
            pltpu.VMEM((depth, width), jnp.bfloat16),
            pltpu.VMEM((4 * rows, width), jnp.bfloat16),
            pltpu.VMEM((4 * rows, width), jnp.bfloat16),
            pltpu.VMEM((2 * rows, 4 * rows), jnp.bfloat16),
            pltpu.VMEM((2 * rows, 4 * rows), jnp.bfloat16),
            pltpu.VMEM((rows, width), jnp.float32),
            pltpu.VMEM((rows, width), jnp.float32),
            pltpu.VMEM((rows, width), jnp.bfloat16),
            pltpu.VMEM((rows, width), jnp.bfloat16),
            pltpu.VMEM((rows, width), jnp.bfloat16),
            pltpu.VMEM((rows, width), jnp.bfloat16),
            pltpu.VMEM((rows, width), jnp.bfloat16),
            pltpu.VMEM((8, rows), jnp.float32),
            pltpu.VMEM((8, rows), jnp.float32),
            dma((4,)),
            dma((COPIES,)),
            dma((COPIES,)),
            dma((COPIES,)),
            dma((COPIES,)),
            dma((count + 1,)),
            dma((count + 1,)),
            dma((count,)),
            dma((count,)),
            *dp_scratch,
        ],
        compiler_params=pltpu.CompilerParams(
            collective_id=0, has_side_effects=True, vmem_limit_bytes=32 * 1024 * 1024
        ),
    )(
        logit_scale.reshape((1,)),
        logit_bias.reshape((1,)),
        *(
            pltpu.with_memory_space_constraint(a, pltpu.HBM)
            for a in (image_of_pair, image_raw, text_feat, text_head)
        ),
    )
    return pl.pallas_call(
        store,
        out_shape=results,
        in_specs=[vmem, vmem],
        out_specs=(hbm, hbm),
        scratch_shapes=[dma((2,))],
        compiler_params=pltpu.CompilerParams(vmem_limit_bytes=4 * 1024 * 1024),
    )(*gradients)


def solution(mesh):
    placed = (P("dp", "loop", None), P("dp", "loop", None), P(), P("dp", "loop"), P(), P())
    return jax.shard_map(
        functools.partial(shards, mesh.shape["dp"]),
        mesh=mesh,
        in_specs=placed,
        out_specs=(P("dp", "loop", None), P("loop", "dp", None)),
        check_vma=False,
    )
```

```python
import functools

import jax
import jax.numpy as jnp
from jax import lax
from jax.experimental import pallas as pl
from jax.experimental.pallas import tpu as pltpu
from jax.sharding import PartitionSpec as P

EPS = 1e-06
CORE, NEAR, FAR = 1, 2, 4
NT = (((1,), (1,)), ((), ()))


def partner(me, mask):
    bit = lax.rem(lax.div(me, mask), 2)
    return me + mask * (1 - 2 * bit)


class Spread:
    def __init__(self, buf, send, recv, me, rows, mask):
        def copy(at, source, target, device, first, count):
            return pltpu.make_async_remote_copy(
                src_ref=buf.at[pl.ds(source * rows + first, count)],
                dst_ref=buf.at[pl.ds(target * rows + first, count)],
                send_sem=send.at[at],
                recv_sem=recv.at[at],
                device_id={"loop": device},
                device_id_type=pl.DeviceIdType.MESH,
            )

        core, side = partner(me, CORE), partner(me, mask)
        piece = rows // STEPS
        self.own_core = copy(0, 0, 1, core, 0, rows)
        self.direct = [copy(1 + i, 0, 2, side, i * piece, piece) for i in range(STEPS)]
        self.relay = [copy(1 + STEPS + i, 2, 3, core, i * piece, piece) for i in range(STEPS)]

    def start(self):
        for c in self.direct:
            c.start()
        self.own_core.start()

    def hand_on(self, i):
        self.direct[i].wait_recv()
        self.relay[i].start()

    def drain(self):
        for c in [self.own_core] + self.direct + self.relay:
            c.wait_send()


STEPS = 4
COPIES = 1 + 2 * STEPS
LAG = 2


class Line:
    def __init__(self, refs, owner, label_row, pieces):
        self.label_out, self.label_in, self.pair_in, self.table_out, self.table_in, self.hot, self.send, self.recv = refs
        self.label_row = label_row
        self.images = self.table_out.shape[1]
        self.pieces = pieces
        self.count = len(pieces)
        self.is_end = owner * (3 - owner) == 0
        self.is_inner = owner * (3 - owner) != 0
        self.inner = 1 + lax.div(owner, 3)
        self.end = (owner - 1) * 3
        self.owner, self.far_inner, self.far_end = owner, 3 - owner, 3 - self.end
        self.label_out[...] = jnp.broadcast_to(label_row, self.label_out.shape)
        self.labels = self.copy(0, self.label_out, self.label_in, self.inner)

    def copy(self, at, source, target, device):
        return pltpu.make_async_remote_copy(
            src_ref=source,
            dst_ref=target,
            send_sem=self.send.at[at],
            recv_sem=self.recv.at[at],
            device_id={"dp": device},
            device_id_type=pl.DeviceIdType.MESH,
        )

    def rows_copy(self, pair_v, k):
        part = (slice(None), pl.ds(*self.pieces[k]))
        return self.copy(1 + k, pair_v.at[part], self.pair_in.at[part], self.inner)

    def table_copy(self, slot, k):
        part = (slot, slice(None), pl.ds(*self.pieces[k]))
        device = (self.end, self.far_inner, self.far_end)[slot]
        at = 1 + (1 + slot) * self.count + k
        return self.copy(at, self.table_out.at[part], self.table_in.at[part], device)

    def mark(self, at, label_row, devices):
        images, rows = self.images, label_row.shape[1]
        ids = lax.broadcasted_iota(jnp.int32, (images, rows), 0).astype(jnp.float32)
        for i, device in enumerate(devices):
            hot = jnp.where(ids + (device * images).astype(jnp.float32) == label_row, 1.0, 0.0)
            self.hot[pl.ds((at + i) * images, images)] = hot.astype(jnp.bfloat16)

    def tables(self, at, count, values):
        hot = self.hot[pl.ds(at * self.images, count * self.images)]
        return jnp.dot(hot, values, preferred_element_type=jnp.float32)

    def prepare(self):
        @pl.when(self.is_end)
        def _():
            self.mark(0, self.label_row, [self.owner])

        @pl.when(self.is_inner)
        def _():
            devices = [self.far_inner, self.far_end, self.owner]
            self.mark(0, self.label_row, [self.end] + devices)
            self.labels.wait_recv()
            self.mark(4, self.label_in[pl.ds(0, 1)], devices)

    def send_labels(self):
        @pl.when(self.is_end)
        def _():
            self.labels.start()

    def ready(self, pair_v, k, d_image_ref):
        part = pl.ds(*self.pieces[k])

        @pl.when(self.is_end)
        def _():
            self.rows_copy(pair_v, k).start()
            d_image_ref[0, :, part] = self.tables(0, 1, pair_v[:, part])

        @pl.when(self.is_inner)
        def _():
            self.table_out[0, :, part] = self.tables(0, 1, pair_v[:, part]).astype(jnp.bfloat16)
            self.table_copy(0, k).start()

    def step(self, pair_v, k, d_image_ref):
        images = self.images
        part = pl.ds(*self.pieces[k])

        @pl.when(self.is_inner)
        def _():
            sums = self.tables(1, 3, pair_v[:, part])
            self.rows_copy(pair_v, k).wait_recv()
            sums = sums + self.tables(4, 3, self.pair_in[:, part])
            for slot in (1, 2):
                self.table_out[slot, :, part] = sums[(slot - 1) * images : slot * images].astype(jnp.bfloat16)
                self.table_copy(slot, k).start()
            d_image_ref[0, :, part] = sums[2 * images :]

    def last(self, pair_v, d_image_ref):
        @pl.when(self.is_end)
        def _():
            for k, piece in enumerate(self.pieces):
                part = pl.ds(*piece)
                self.table_copy(0, k).wait_recv()
                self.table_copy(2, k).wait_recv()
                d_image_ref[0, :, part] += (
                    self.table_in[0, :, part].astype(jnp.float32) + self.table_in[2, :, part].astype(jnp.float32)
                )
            self.labels.wait_send()
            for k in range(self.count):
                self.rows_copy(pair_v, k).wait_send()

        @pl.when(self.is_inner)
        def _():
            for k, piece in enumerate(self.pieces):
                part = pl.ds(*piece)
                self.table_copy(1, k).wait_recv()
                d_image_ref[0, :, part] += self.table_in[1, :, part].astype(jnp.float32)
            for k in range(self.count):
                for slot in range(3):
                    self.table_copy(slot, k).wait_send()


class Direct:
    def __init__(self, refs, owner, label_row, owners):
        self.table_out, self.table_in, self.send, self.recv = refs
        self.owner, self.label_row, self.owners = owner, label_row, owners

    def copy(self, apart):
        return pltpu.make_async_remote_copy(
            src_ref=self.table_out.at[apart],
            dst_ref=self.table_in.at[apart],
            send_sem=self.send.at[apart],
            recv_sem=self.recv.at[apart],
            device_id={"dp": lax.rem(self.owner + apart, self.owners)},
            device_id_type=pl.DeviceIdType.MESH,
        )

    def table(self, pair_v, apart):
        images, rows = self.table_out.shape[1], self.label_row.shape[1]
        first = lax.rem(self.owner + apart, self.owners) * images
        ids = lax.broadcasted_iota(jnp.int32, (images, rows), 0) + first
        onehot = jnp.where(ids.astype(jnp.float32) == self.label_row, 1.0, 0.0).astype(jnp.bfloat16)
        return jnp.dot(onehot, pair_v[...], preferred_element_type=jnp.float32)

    def send_labels(self):
        pass

    def prepare(self):
        pass

    def ready(self, pair_v, k, d_image_ref):
        if k + 1 < len(pieces_of(pair_v.shape[1])):
            return
        for apart in range(1, self.owners):
            self.table_out[apart] = self.table(pair_v, apart).astype(jnp.bfloat16)
            self.copy(apart).start()
        d_image_ref[0] = self.table(pair_v, 0)

    def step(self, pair_v, k, d_image_ref):
        pass

    def last(self, pair_v, d_image_ref):
        for apart in range(1, self.owners):
            self.copy(apart).wait_recv()
            d_image_ref[0] += self.table_in[apart].astype(jnp.float32)
        for apart in range(1, self.owners):
            self.copy(apart).wait_send()


def pieces_of(width):
    lanes = width // 128
    sizes = [1] + [2] * ((lanes - 3) // 2) + [1] * (2 - lanes % 2 + 1) if lanes > 3 else [1] * lanes
    return [(128 * sum(sizes[:i]), 128 * size) for i, size in enumerate(sizes)]


def kernel(
    owners,
    scale_ref,
    shift_ref,
    label_ref,
    image_ref,
    feat_ref,
    head_ref,
    d_feat_ref,
    d_image_ref,
    label_v,
    image_v,
    feat_v,
    head_v,
    xbuf,
    ybuf,
    x_weight,
    y_weight,
    unit_y_v,
    text_v,
    image_grad_v,
    d_pair_v,
    x_out,
    x_in,
    y_out,
    y_in,
    dots_out,
    dots_in,
    load_sem,
    x_send,
    x_recv,
    y_send,
    y_recv,
    px_send,
    px_recv,
    py_send,
    py_recv,
    *dp_refs,
):
    rows, width = image_v.shape
    me = lax.axis_index("loop")
    owner = lax.axis_index("dp")

    barrier = pltpu.get_barrier_semaphore()
    for mask in (CORE, NEAR, FAR):
        pl.semaphore_signal(
            barrier, inc=1, device_id={"loop": partner(me, mask)}, device_id_type=pl.DeviceIdType.MESH
        )
    for apart in range(1, owners):
        pl.semaphore_signal(
            barrier,
            inc=1,
            device_id={"dp": lax.rem(owner + apart, owners)},
            device_id_type=pl.DeviceIdType.MESH,
        )

    load_image = pltpu.make_async_copy(image_ref.at[0], image_v, load_sem.at[0])
    load_feat = pltpu.make_async_copy(feat_ref.at[0], feat_v, load_sem.at[1])
    load_head = pltpu.make_async_copy(head_ref, head_v, load_sem.at[2])
    load_label = pltpu.make_async_copy(label_ref, label_v, load_sem.at[3])
    load_label.start()
    load_image.start()
    load_feat.start()
    load_head.start()

    scale = scale_ref[0]
    shift = shift_ref[0]
    load_label.wait()
    label_row = label_v[...].astype(jnp.float32)
    label_grid = jnp.broadcast_to(label_row, (rows, rows))
    same = label_grid == label_grid.T

    xs = Spread(xbuf, x_send, x_recv, me, rows, NEAR)
    ys = Spread(ybuf, y_send, y_recv, me, rows, FAR)
    pieces = pieces_of(width)
    if owners == 4:
        sums = Line(dp_refs, owner, label_row, pieces)
    else:
        sums = Direct(dp_refs, owner, label_row, owners)

    def side_copy(source, target, send, recv, at, mask):
        return pltpu.make_async_remote_copy(
            src_ref=source,
            dst_ref=target,
            send_sem=send.at[at],
            recv_sem=recv.at[at],
            device_id={"loop": partner(me, mask)},
            device_id_type=pl.DeviceIdType.MESH,
        )

    columns = [(slice(None), pl.ds(*piece)) for piece in pieces]
    x_parts = [side_copy(x_out.at[c], x_in.at[c], px_send, px_recv, k, NEAR) for k, c in enumerate(columns)]
    y_parts = [side_copy(y_out.at[c], y_in.at[c], py_send, py_recv, k, FAR) for k, c in enumerate(columns)]
    dots_copy = side_copy(dots_out, dots_in, px_send, px_recv, len(pieces), NEAR)

    load_image.wait()
    image = image_v[...].astype(jnp.float32)
    inv_x = lax.rsqrt(jnp.sum(image * image, axis=-1, keepdims=True) + EPS)
    xbuf[pl.ds(0, rows)] = (image * inv_x).astype(jnp.bfloat16)

    load_feat.wait()
    load_head.wait()
    text_pre = jnp.dot(feat_v[...], head_v[...], preferred_element_type=jnp.float32)
    inv_y = lax.rsqrt(jnp.sum(text_pre * text_pre, axis=-1, keepdims=True) + EPS)
    unit_y = text_pre * inv_y
    ybuf[pl.ds(0, rows)] = unit_y.astype(jnp.bfloat16)
    pl.semaphore_wait(barrier, 3 + owners - 1)
    ys.start()
    xs.start()
    sums.send_labels()
    unit_y_v[...] = unit_y

    def weights(mine, row, other, block, blocks, weight):
        dots = lax.dot_general(
            mine[pl.ds(row * 2 * rows, rows)],
            other[pl.ds(block * rows, blocks * rows)],
            NT,
            preferred_element_type=jnp.float32,
        )
        logits = scale * dots + shift
        if row == 0 and block == 0:
            flip = jnp.concatenate([same, jnp.zeros_like(same)], axis=1)
            value = jax.nn.sigmoid(jnp.where(flip, -logits, logits))
            value = jnp.where(flip, -value, value)
        else:
            value = jax.nn.sigmoid(logits)
        value = value.astype(jnp.bfloat16)
        weight[pl.ds(row * rows, rows), pl.ds(block * rows, blocks * rows)] = value
        return value.astype(jnp.float32) * dots

    def product(weight, row, buf, column):
        return jnp.dot(weight[pl.ds(row * rows, rows)], buf[column], preferred_element_type=jnp.float32)

    everything = (slice(None), slice(None))

    ys.own_core.wait_recv()
    xs.own_core.wait_recv()
    own_dots = weights(xbuf, 0, ybuf, 0, 2, x_weight)
    ys.hand_on(0)
    xs.hand_on(0)
    weights(ybuf, 0, xbuf, 0, 2, y_weight)
    for i in range(1, STEPS):
        ys.hand_on(i)
        xs.hand_on(i)
    near_dots = weights(xbuf, 1, ybuf, 0, 2, x_weight)

    for c in ys.relay:
        c.wait_recv()
    near_dots = jnp.sum(near_dots + weights(xbuf, 1, ybuf, 2, 2, x_weight), axis=-1, keepdims=True)
    dots_out[...] = jnp.broadcast_to(near_dots, (rows, rows)).T[:8]
    dots_copy.start()
    for first in range(0, len(pieces), 2):
        pair = pieces[first : first + 2]
        part = (slice(None), pl.ds(pair[0][0], sum(size for _, size in pair)))
        x_out[part] = product(x_weight, 1, ybuf, part).astype(jnp.bfloat16)
        for c in x_parts[first : first + 2]:
            c.start()

    own_dots = jnp.sum(own_dots + weights(xbuf, 0, ybuf, 2, 2, x_weight), axis=-1, keepdims=True)
    image_grad_v[...] = product(x_weight, 0, ybuf, everything)
    sums.prepare()
    dots_copy.wait_recv()
    there = jnp.broadcast_to(dots_in[pl.ds(0, 1)], (rows, rows)).T[:, :1]
    along = scale * (own_dots + there)

    def far_texts():
        for c in xs.relay:
            c.wait_recv()
        weights(ybuf, 1, xbuf, 0, 4, y_weight)
        y_out[...] = product(y_weight, 1, xbuf, everything).astype(jnp.bfloat16)
        for c in y_parts:
            c.start()

    def own_texts():
        weights(ybuf, 0, xbuf, 2, 2, y_weight)
        text_v[...] = product(y_weight, 0, xbuf, everything)

    fill = {1: far_texts, len(pieces) - 3: own_texts}
    for k, c in enumerate(columns):
        unit_x = image_v[c].astype(jnp.float32) * inv_x
        x_parts[k].wait_recv()
        grad = scale * (image_grad_v[c] + x_in[c].astype(jnp.float32))
        d_pair_v[c] = ((grad - unit_x * along) * inv_x).astype(jnp.bfloat16)
        sums.ready(d_pair_v, k, d_image_ref)
        if k in fill:
            fill[k]()
        if k >= LAG:
            sums.step(d_pair_v, k - LAG, d_image_ref)

    for k in range(len(pieces) - LAG, len(pieces)):
        sums.step(d_pair_v, k, d_image_ref)
    for c in y_parts:
        c.wait_recv()
    grad = scale * (text_v[...] + y_in[...].astype(jnp.float32))
    unit_y = unit_y_v[...]
    d_text = (grad - unit_y * jnp.sum(unit_y * grad, axis=-1, keepdims=True)) * inv_y
    d_feat_ref[0] = lax.dot_general(
        d_text.astype(jnp.bfloat16), head_v[...], NT, preferred_element_type=jnp.float32
    )

    sums.last(d_pair_v, d_image_ref)
    xs.drain()
    ys.drain()
    for c in x_parts + y_parts + [dots_copy]:
        c.wait_send()


def store(feat_v, image_v, d_feat_ref, d_image_ref, sem):
    feat = pltpu.make_async_copy(feat_v, d_feat_ref, sem.at[0])
    image = pltpu.make_async_copy(image_v, d_image_ref, sem.at[1])
    feat.start()
    image.start()
    feat.wait()
    image.wait()


def shards(owners, image_raw, text_feat, text_head, image_of_pair, logit_scale, logit_bias):
    _, rows, width = image_raw.shape
    depth = text_head.shape[0]
    images = rows // 2
    hbm = pl.BlockSpec(memory_space=pltpu.HBM)
    scalar = pl.BlockSpec(memory_space=pltpu.SMEM)
    vmem = pl.BlockSpec(memory_space=pltpu.VMEM)
    dma = pltpu.SemaphoreType.DMA
    count = len(pieces_of(width))
    if owners == 4:
        dp_scratch = [
            pltpu.VMEM((8, rows), jnp.float32),
            pltpu.VMEM((8, rows), jnp.float32),
            pltpu.VMEM((rows, width), jnp.bfloat16),
            pltpu.VMEM((3, images, width), jnp.bfloat16),
            pltpu.VMEM((3, images, width), jnp.bfloat16),
            pltpu.VMEM((7 * images, rows), jnp.bfloat16),
            dma((1 + 4 * count,)),
            dma((1 + 4 * count,)),
        ]
    else:
        dp_scratch = [
            pltpu.VMEM((owners, images, width), jnp.bfloat16),
            pltpu.VMEM((owners, images, width), jnp.bfloat16),
            dma((owners,)),
            dma((owners,)),
        ]
    results = (
        jax.ShapeDtypeStruct((1, rows, depth), jnp.float32),
        jax.ShapeDtypeStruct((1, images, width), jnp.float32),
    )
    gradients = pl.pallas_call(
        functools.partial(kernel, owners),
        out_shape=results,
        in_specs=[scalar, scalar, hbm, hbm, hbm, hbm],
        out_specs=(vmem, vmem),
        scratch_shapes=[
            pltpu.VMEM((1, rows), jnp.int32),
            pltpu.VMEM((rows, width), jnp.bfloat16),
            pltpu.VMEM((rows, depth), jnp.bfloat16),
            pltpu.VMEM((depth, width), jnp.bfloat16),
            pltpu.VMEM((4 * rows, width), jnp.bfloat16),
            pltpu.VMEM((4 * rows, width), jnp.bfloat16),
            pltpu.VMEM((2 * rows, 4 * rows), jnp.bfloat16),
            pltpu.VMEM((2 * rows, 4 * rows), jnp.bfloat16),
            pltpu.VMEM((rows, width), jnp.float32),
            pltpu.VMEM((rows, width), jnp.float32),
            pltpu.VMEM((rows, width), jnp.float32),
            pltpu.VMEM((rows, width), jnp.bfloat16),
            pltpu.VMEM((rows, width), jnp.bfloat16),
            pltpu.VMEM((rows, width), jnp.bfloat16),
            pltpu.VMEM((rows, width), jnp.bfloat16),
            pltpu.VMEM((rows, width), jnp.bfloat16),
            pltpu.VMEM((8, rows), jnp.float32),
            pltpu.VMEM((8, rows), jnp.float32),
            dma((4,)),
            dma((COPIES,)),
            dma((COPIES,)),
            dma((COPIES,)),
            dma((COPIES,)),
            dma((count + 1,)),
            dma((count + 1,)),
            dma((count,)),
            dma((count,)),
            *dp_scratch,
        ],
        compiler_params=pltpu.CompilerParams(
            collective_id=0, has_side_effects=True, vmem_limit_bytes=32 * 1024 * 1024
        ),
    )(
        logit_scale.reshape((1,)),
        logit_bias.reshape((1,)),
        *(
            pltpu.with_memory_space_constraint(a, pltpu.HBM)
            for a in (image_of_pair, image_raw, text_feat, text_head)
        ),
    )
    return pl.pallas_call(
        store,
        out_shape=results,
        in_specs=[vmem, vmem],
        out_specs=(hbm, hbm),
        scratch_shapes=[dma((2,))],
        compiler_params=pltpu.CompilerParams(vmem_limit_bytes=4 * 1024 * 1024),
    )(*gradients)


def solution(mesh):
    placed = (P("dp", "loop", None), P("dp", "loop", None), P(), P("dp", "loop"), P(), P())
    return jax.shard_map(
        functools.partial(shards, mesh.shape["dp"]),
        mesh=mesh,
        in_specs=placed,
        out_specs=(P("dp", "loop", None), P("loop", "dp", None)),
        check_vma=False,
    )
```

```python
import functools

import jax
import jax.numpy as jnp
from jax import lax
from jax.experimental import pallas as pl
from jax.experimental.pallas import tpu as pltpu
from jax.sharding import PartitionSpec as P

EPS = 1e-06
CORE, NEAR, FAR = 1, 2, 4
NT = (((1,), (1,)), ((), ()))


def partner(me, mask):
    bit = lax.rem(lax.div(me, mask), 2)
    return me + mask * (1 - 2 * bit)


class Spread:
    def __init__(self, buf, send, recv, me, rows, mask):
        def copy(at, source, target, device, first, count):
            return pltpu.make_async_remote_copy(
                src_ref=buf.at[pl.ds(source * rows + first, count)],
                dst_ref=buf.at[pl.ds(target * rows + first, count)],
                send_sem=send.at[at],
                recv_sem=recv.at[at],
                device_id={"loop": device},
                device_id_type=pl.DeviceIdType.MESH,
            )

        core, side = partner(me, CORE), partner(me, mask)
        piece = rows // STEPS
        self.own_core = copy(0, 0, 1, core, 0, rows)
        self.direct = [copy(1 + i, 0, 2, side, i * piece, piece) for i in range(STEPS)]
        self.relay = [copy(1 + STEPS + i, 2, 3, core, i * piece, piece) for i in range(STEPS)]

    def start(self):
        for c in self.direct:
            c.start()
        self.own_core.start()

    def hand_on(self, i):
        self.direct[i].wait_recv()
        self.relay[i].start()

    def drain(self):
        for c in [self.own_core] + self.direct + self.relay:
            c.wait_send()


STEPS = 4
COPIES = 1 + 2 * STEPS
LAG = 2


class Line:
    def __init__(self, refs, owner, label_row, pieces):
        self.label_out, self.label_in, self.pair_in, self.table_out, self.table_in, self.hot, self.send, self.recv = refs
        self.label_row = label_row
        self.images = self.table_out.shape[1]
        self.pieces = pieces
        self.count = len(pieces)
        self.is_end = owner * (3 - owner) == 0
        self.is_inner = owner * (3 - owner) != 0
        self.inner = 1 + lax.div(owner, 3)
        self.end = (owner - 1) * 3
        self.owner, self.far_inner, self.far_end = owner, 3 - owner, 3 - self.end
        self.label_out[...] = jnp.broadcast_to(label_row, self.label_out.shape)
        self.labels = self.copy(0, self.label_out, self.label_in, self.inner)

    def copy(self, at, source, target, device):
        return pltpu.make_async_remote_copy(
            src_ref=source,
            dst_ref=target,
            send_sem=self.send.at[at],
            recv_sem=self.recv.at[at],
            device_id={"dp": device},
            device_id_type=pl.DeviceIdType.MESH,
        )

    def rows_copy(self, pair_v, k):
        part = (slice(None), pl.ds(*self.pieces[k]))
        return self.copy(1 + k, pair_v.at[part], self.pair_in.at[part], self.inner)

    def table_copy(self, slot, k):
        part = (slot, slice(None), pl.ds(*self.pieces[k]))
        device = (self.end, self.far_inner, self.far_end)[slot]
        at = 1 + (1 + slot) * self.count + k
        return self.copy(at, self.table_out.at[part], self.table_in.at[part], device)

    def mark(self, at, label_row, devices):
        images, rows = self.images, label_row.shape[1]
        ids = lax.broadcasted_iota(jnp.int32, (images, rows), 0).astype(jnp.float32)
        for i, device in enumerate(devices):
            hot = jnp.where(ids + (device * images).astype(jnp.float32) == label_row, 1.0, 0.0)
            self.hot[pl.ds((at + i) * images, images)] = hot.astype(jnp.bfloat16)

    def tables(self, at, count, values):
        hot = self.hot[pl.ds(at * self.images, count * self.images)]
        return jnp.dot(hot, values, preferred_element_type=jnp.float32)

    def prepare(self):
        @pl.when(self.is_end)
        def _():
            self.mark(0, self.label_row, [self.owner])

        @pl.when(self.is_inner)
        def _():
            devices = [self.far_inner, self.far_end, self.owner]
            self.mark(0, self.label_row, [self.end] + devices)
            self.labels.wait_recv()
            self.mark(4, self.label_in[pl.ds(0, 1)], devices)

    def send_labels(self):
        @pl.when(self.is_end)
        def _():
            self.labels.start()

    def ready(self, pair_v, k, d_image_ref):
        part = pl.ds(*self.pieces[k])

        @pl.when(self.is_end)
        def _():
            self.rows_copy(pair_v, k).start()
            d_image_ref[0, :, part] = self.tables(0, 1, pair_v[:, part])

        @pl.when(self.is_inner)
        def _():
            self.table_out[0, :, part] = self.tables(0, 1, pair_v[:, part]).astype(jnp.bfloat16)
            self.table_copy(0, k).start()

    def step(self, pair_v, k, d_image_ref):
        images = self.images
        part = pl.ds(*self.pieces[k])

        @pl.when(self.is_inner)
        def _():
            sums = self.tables(1, 3, pair_v[:, part])
            self.rows_copy(pair_v, k).wait_recv()
            sums = sums + self.tables(4, 3, self.pair_in[:, part])
            for slot in (1, 2):
                self.table_out[slot, :, part] = sums[(slot - 1) * images : slot * images].astype(jnp.bfloat16)
                self.table_copy(slot, k).start()
            d_image_ref[0, :, part] = sums[2 * images :]

    def last(self, pair_v, d_image_ref):
        @pl.when(self.is_end)
        def _():
            for k, piece in enumerate(self.pieces):
                part = pl.ds(*piece)
                self.table_copy(0, k).wait_recv()
                self.table_copy(2, k).wait_recv()
                d_image_ref[0, :, part] += (
                    self.table_in[0, :, part].astype(jnp.float32) + self.table_in[2, :, part].astype(jnp.float32)
                )
            self.labels.wait_send()
            for k in range(self.count):
                self.rows_copy(pair_v, k).wait_send()

        @pl.when(self.is_inner)
        def _():
            for k, piece in enumerate(self.pieces):
                part = pl.ds(*piece)
                self.table_copy(1, k).wait_recv()
                d_image_ref[0, :, part] += self.table_in[1, :, part].astype(jnp.float32)
            for k in range(self.count):
                for slot in range(3):
                    self.table_copy(slot, k).wait_send()


class Direct:
    def __init__(self, refs, owner, label_row, owners):
        self.table_out, self.table_in, self.send, self.recv = refs
        self.owner, self.label_row, self.owners = owner, label_row, owners

    def copy(self, apart):
        return pltpu.make_async_remote_copy(
            src_ref=self.table_out.at[apart],
            dst_ref=self.table_in.at[apart],
            send_sem=self.send.at[apart],
            recv_sem=self.recv.at[apart],
            device_id={"dp": lax.rem(self.owner + apart, self.owners)},
            device_id_type=pl.DeviceIdType.MESH,
        )

    def table(self, pair_v, apart):
        images, rows = self.table_out.shape[1], self.label_row.shape[1]
        first = lax.rem(self.owner + apart, self.owners) * images
        ids = lax.broadcasted_iota(jnp.int32, (images, rows), 0) + first
        onehot = jnp.where(ids.astype(jnp.float32) == self.label_row, 1.0, 0.0).astype(jnp.bfloat16)
        return jnp.dot(onehot, pair_v[...], preferred_element_type=jnp.float32)

    def send_labels(self):
        pass

    def prepare(self):
        pass

    def ready(self, pair_v, k, d_image_ref):
        if k + 1 < len(pieces_of(pair_v.shape[1])):
            return
        for apart in range(1, self.owners):
            self.table_out[apart] = self.table(pair_v, apart).astype(jnp.bfloat16)
            self.copy(apart).start()
        d_image_ref[0] = self.table(pair_v, 0)

    def step(self, pair_v, k, d_image_ref):
        pass

    def last(self, pair_v, d_image_ref):
        for apart in range(1, self.owners):
            self.copy(apart).wait_recv()
            d_image_ref[0] += self.table_in[apart].astype(jnp.float32)
        for apart in range(1, self.owners):
            self.copy(apart).wait_send()


def pieces_of(width):
    lanes = width // 128
    sizes = [1] + [2] * ((lanes - 3) // 2) + [1] * (2 - lanes % 2 + 1) if lanes > 3 else [1] * lanes
    return [(128 * sum(sizes[:i]), 128 * size) for i, size in enumerate(sizes)]


def kernel(
    owners,
    scale_ref,
    shift_ref,
    label_ref,
    image_ref,
    feat_ref,
    head_ref,
    d_feat_ref,
    d_image_ref,
    label_v,
    image_v,
    feat_v,
    head_v,
    xbuf,
    ybuf,
    x_weight,
    y_weight,
    unit_y_v,
    text_v,
    image_grad_v,
    d_pair_v,
    x_out,
    x_in,
    y_out,
    y_in,
    dots_out,
    dots_in,
    text_dots_out,
    text_dots_in,
    load_sem,
    x_send,
    x_recv,
    y_send,
    y_recv,
    px_send,
    px_recv,
    py_send,
    py_recv,
    *dp_refs,
):
    rows, width = image_v.shape
    me = lax.axis_index("loop")
    owner = lax.axis_index("dp")

    barrier = pltpu.get_barrier_semaphore()
    for mask in (CORE, NEAR, FAR):
        pl.semaphore_signal(
            barrier, inc=1, device_id={"loop": partner(me, mask)}, device_id_type=pl.DeviceIdType.MESH
        )
    for apart in range(1, owners):
        pl.semaphore_signal(
            barrier,
            inc=1,
            device_id={"dp": lax.rem(owner + apart, owners)},
            device_id_type=pl.DeviceIdType.MESH,
        )

    load_image = pltpu.make_async_copy(image_ref.at[0], image_v, load_sem.at[0])
    load_feat = pltpu.make_async_copy(feat_ref.at[0], feat_v, load_sem.at[1])
    load_head = pltpu.make_async_copy(head_ref, head_v, load_sem.at[2])
    load_label = pltpu.make_async_copy(label_ref, label_v, load_sem.at[3])
    load_label.start()
    load_image.start()
    load_feat.start()
    load_head.start()

    scale = scale_ref[0]
    shift = shift_ref[0]
    load_label.wait()
    label_row = label_v[...].astype(jnp.float32)
    label_grid = jnp.broadcast_to(label_row, (rows, rows))
    same = label_grid == label_grid.T

    xs = Spread(xbuf, x_send, x_recv, me, rows, NEAR)
    ys = Spread(ybuf, y_send, y_recv, me, rows, FAR)
    pieces = pieces_of(width)
    if owners == 4:
        sums = Line(dp_refs, owner, label_row, pieces)
    else:
        sums = Direct(dp_refs, owner, label_row, owners)

    def side_copy(source, target, send, recv, at, mask):
        return pltpu.make_async_remote_copy(
            src_ref=source,
            dst_ref=target,
            send_sem=send.at[at],
            recv_sem=recv.at[at],
            device_id={"loop": partner(me, mask)},
            device_id_type=pl.DeviceIdType.MESH,
        )

    columns = [(slice(None), pl.ds(*piece)) for piece in pieces]
    x_parts = [side_copy(x_out.at[c], x_in.at[c], px_send, px_recv, k, NEAR) for k, c in enumerate(columns)]
    y_parts = [side_copy(y_out.at[c], y_in.at[c], py_send, py_recv, k, FAR) for k, c in enumerate(columns)]
    dots_copy = side_copy(dots_out, dots_in, px_send, px_recv, len(pieces), NEAR)
    text_dots_copy = side_copy(text_dots_out, text_dots_in, py_send, py_recv, len(pieces), FAR)

    load_image.wait()
    image = image_v[...].astype(jnp.float32)
    inv_x = lax.rsqrt(jnp.sum(image * image, axis=-1, keepdims=True) + EPS)
    xbuf[pl.ds(0, rows)] = (image * inv_x).astype(jnp.bfloat16)

    load_feat.wait()
    load_head.wait()
    text_pre = jnp.dot(feat_v[...], head_v[...], preferred_element_type=jnp.float32)
    inv_y = lax.rsqrt(jnp.sum(text_pre * text_pre, axis=-1, keepdims=True) + EPS)
    unit_y = text_pre * inv_y
    ybuf[pl.ds(0, rows)] = unit_y.astype(jnp.bfloat16)
    pl.semaphore_wait(barrier, 3 + owners - 1)
    ys.start()
    xs.start()
    sums.send_labels()
    unit_y_v[...] = unit_y

    def weights(mine, row, other, block, blocks, weight):
        dots = lax.dot_general(
            mine[pl.ds(row * 2 * rows, rows)],
            other[pl.ds(block * rows, blocks * rows)],
            NT,
            preferred_element_type=jnp.float32,
        )
        logits = scale * dots + shift
        if row == 0 and block == 0:
            flip = jnp.concatenate([same, jnp.zeros_like(same)], axis=1)
            value = jax.nn.sigmoid(jnp.where(flip, -logits, logits))
            value = jnp.where(flip, -value, value)
        else:
            value = jax.nn.sigmoid(logits)
        value = value.astype(jnp.bfloat16)
        weight[pl.ds(row * rows, rows), pl.ds(block * rows, blocks * rows)] = value
        return value.astype(jnp.float32) * dots

    def product(weight, row, buf, column):
        return jnp.dot(weight[pl.ds(row * rows, rows)], buf[column], preferred_element_type=jnp.float32)

    everything = (slice(None), slice(None))

    ys.own_core.wait_recv()
    xs.own_core.wait_recv()
    own_dots = weights(xbuf, 0, ybuf, 0, 2, x_weight)
    ys.hand_on(0)
    xs.hand_on(0)
    own_text_dots = [weights(ybuf, 0, xbuf, 0, 2, y_weight)]
    for i in range(1, STEPS):
        ys.hand_on(i)
        xs.hand_on(i)
    near_dots = weights(xbuf, 1, ybuf, 0, 2, x_weight)
    far_dots = weights(ybuf, 1, xbuf, 0, 2, y_weight)

    for c in ys.relay:
        c.wait_recv()
    near_dots = jnp.sum(near_dots + weights(xbuf, 1, ybuf, 2, 2, x_weight), axis=-1, keepdims=True)
    dots_out[...] = jnp.broadcast_to(near_dots, (rows, rows)).T[:8]
    dots_copy.start()
    for first in range(0, len(pieces), 2):
        pair = pieces[first : first + 2]
        part = (slice(None), pl.ds(pair[0][0], sum(size for _, size in pair)))
        x_out[part] = product(x_weight, 1, ybuf, part).astype(jnp.bfloat16)
        for c in x_parts[first : first + 2]:
            c.start()

    own_dots = jnp.sum(own_dots + weights(xbuf, 0, ybuf, 2, 2, x_weight), axis=-1, keepdims=True)
    image_grad_v[...] = product(x_weight, 0, ybuf, everything)
    sums.prepare()
    dots_copy.wait_recv()
    there = jnp.broadcast_to(dots_in[pl.ds(0, 1)], (rows, rows)).T[:, :1]
    along = scale * (own_dots + there)

    def far_texts():
        for c in xs.relay:
            c.wait_recv()
        dots = jnp.sum(far_dots + weights(ybuf, 1, xbuf, 2, 2, y_weight), axis=-1, keepdims=True)
        text_dots_out[...] = jnp.broadcast_to(dots, (rows, rows)).T[:8]
        text_dots_copy.start()
        for first in range(0, len(pieces), 2):
            pair = pieces[first : first + 2]
            part = (slice(None), pl.ds(pair[0][0], sum(size for _, size in pair)))
            y_out[part] = product(y_weight, 1, xbuf, part).astype(jnp.bfloat16)
            for c in y_parts[first : first + 2]:
                c.start()

    def own_texts():
        own_text_dots.append(weights(ybuf, 0, xbuf, 2, 2, y_weight))
        text_v[...] = product(y_weight, 0, xbuf, everything)

    fill = {1: far_texts, len(pieces) - 3: own_texts}
    for k, c in enumerate(columns):
        unit_x = image_v[c].astype(jnp.float32) * inv_x
        x_parts[k].wait_recv()
        grad = scale * (image_grad_v[c] + x_in[c].astype(jnp.float32))
        d_pair_v[c] = ((grad - unit_x * along) * inv_x).astype(jnp.bfloat16)
        sums.ready(d_pair_v, k, d_image_ref)
        if k in fill:
            fill[k]()
        if k >= LAG:
            sums.step(d_pair_v, k - LAG, d_image_ref)

    text_dots_copy.wait_recv()
    there = jnp.broadcast_to(text_dots_in[pl.ds(0, 1)], (rows, rows)).T[:, :1]
    along = scale * (jnp.sum(own_text_dots[0] + own_text_dots[1], axis=-1, keepdims=True) + there)
    steps = {2 * i: len(pieces) - LAG + i for i in range(LAG)}
    for k, c in enumerate(columns):
        y_parts[k].wait_recv()
        grad = scale * (text_v[c] + y_in[c].astype(jnp.float32))
        d_text = ((grad - unit_y_v[c] * along) * inv_y).astype(jnp.bfloat16)
        term = lax.dot_general(d_text, head_v[c], NT, preferred_element_type=jnp.float32)
        if k == 0:
            d_feat_ref[0] = term
        else:
            d_feat_ref[0] += term
        if k in steps:
            sums.step(d_pair_v, steps[k], d_image_ref)

    sums.last(d_pair_v, d_image_ref)
    xs.drain()
    ys.drain()
    for c in x_parts + y_parts + [dots_copy, text_dots_copy]:
        c.wait_send()


def store(feat_v, image_v, d_feat_ref, d_image_ref, sem):
    feat = pltpu.make_async_copy(feat_v, d_feat_ref, sem.at[0])
    image = pltpu.make_async_copy(image_v, d_image_ref, sem.at[1])
    feat.start()
    image.start()
    feat.wait()
    image.wait()


def shards(owners, image_raw, text_feat, text_head, image_of_pair, logit_scale, logit_bias):
    _, rows, width = image_raw.shape
    depth = text_head.shape[0]
    images = rows // 2
    hbm = pl.BlockSpec(memory_space=pltpu.HBM)
    scalar = pl.BlockSpec(memory_space=pltpu.SMEM)
    vmem = pl.BlockSpec(memory_space=pltpu.VMEM)
    dma = pltpu.SemaphoreType.DMA
    count = len(pieces_of(width))
    if owners == 4:
        dp_scratch = [
            pltpu.VMEM((8, rows), jnp.float32),
            pltpu.VMEM((8, rows), jnp.float32),
            pltpu.VMEM((rows, width), jnp.bfloat16),
            pltpu.VMEM((3, images, width), jnp.bfloat16),
            pltpu.VMEM((3, images, width), jnp.bfloat16),
            pltpu.VMEM((7 * images, rows), jnp.bfloat16),
            dma((1 + 4 * count,)),
            dma((1 + 4 * count,)),
        ]
    else:
        dp_scratch = [
            pltpu.VMEM((owners, images, width), jnp.bfloat16),
            pltpu.VMEM((owners, images, width), jnp.bfloat16),
            dma((owners,)),
            dma((owners,)),
        ]
    results = (
        jax.ShapeDtypeStruct((1, rows, depth), jnp.float32),
        jax.ShapeDtypeStruct((1, images, width), jnp.float32),
    )
    gradients = pl.pallas_call(
        functools.partial(kernel, owners),
        out_shape=results,
        in_specs=[scalar, scalar, hbm, hbm, hbm, hbm],
        out_specs=(vmem, vmem),
        scratch_shapes=[
            pltpu.VMEM((1, rows), jnp.int32),
            pltpu.VMEM((rows, width), jnp.bfloat16),
            pltpu.VMEM((rows, depth), jnp.bfloat16),
            pltpu.VMEM((depth, width), jnp.bfloat16),
            pltpu.VMEM((4 * rows, width), jnp.bfloat16),
            pltpu.VMEM((4 * rows, width), jnp.bfloat16),
            pltpu.VMEM((2 * rows, 4 * rows), jnp.bfloat16),
            pltpu.VMEM((2 * rows, 4 * rows), jnp.bfloat16),
            pltpu.VMEM((rows, width), jnp.float32),
            pltpu.VMEM((rows, width), jnp.float32),
            pltpu.VMEM((rows, width), jnp.float32),
            pltpu.VMEM((rows, width), jnp.bfloat16),
            pltpu.VMEM((rows, width), jnp.bfloat16),
            pltpu.VMEM((rows, width), jnp.bfloat16),
            pltpu.VMEM((rows, width), jnp.bfloat16),
            pltpu.VMEM((rows, width), jnp.bfloat16),
            pltpu.VMEM((8, rows), jnp.float32),
            pltpu.VMEM((8, rows), jnp.float32),
            pltpu.VMEM((8, rows), jnp.float32),
            pltpu.VMEM((8, rows), jnp.float32),
            dma((4,)),
            dma((COPIES,)),
            dma((COPIES,)),
            dma((COPIES,)),
            dma((COPIES,)),
            dma((count + 1,)),
            dma((count + 1,)),
            dma((count + 1,)),
            dma((count + 1,)),
            *dp_scratch,
        ],
        compiler_params=pltpu.CompilerParams(
            collective_id=0, has_side_effects=True, vmem_limit_bytes=32 * 1024 * 1024
        ),
    )(
        logit_scale.reshape((1,)),
        logit_bias.reshape((1,)),
        *(
            pltpu.with_memory_space_constraint(a, pltpu.HBM)
            for a in (image_of_pair, image_raw, text_feat, text_head)
        ),
    )
    return pl.pallas_call(
        store,
        out_shape=results,
        in_specs=[vmem, vmem],
        out_specs=(hbm, hbm),
        scratch_shapes=[dma((2,))],
        compiler_params=pltpu.CompilerParams(vmem_limit_bytes=4 * 1024 * 1024),
    )(*gradients)


def solution(mesh):
    placed = (P("dp", "loop", None), P("dp", "loop", None), P(), P("dp", "loop"), P(), P())
    return jax.shard_map(
        functools.partial(shards, mesh.shape["dp"]),
        mesh=mesh,
        in_specs=placed,
        out_specs=(P("dp", "loop", None), P("loop", "dp", None)),
        check_vma=False,
    )
```

```python
import functools

import jax
import jax.numpy as jnp
from jax import lax
from jax.experimental import pallas as pl
from jax.experimental.pallas import tpu as pltpu
from jax.sharding import PartitionSpec as P

EPS = 1e-06
CORE, NEAR, FAR = 1, 2, 4
NT = (((1,), (1,)), ((), ()))


def partner(me, mask):
    bit = lax.rem(lax.div(me, mask), 2)
    return me + mask * (1 - 2 * bit)


class Spread:
    def __init__(self, buf, send, recv, me, rows, mask):
        def copy(at, source, target, device, first, count):
            return pltpu.make_async_remote_copy(
                src_ref=buf.at[pl.ds(source * rows + first, count)],
                dst_ref=buf.at[pl.ds(target * rows + first, count)],
                send_sem=send.at[at],
                recv_sem=recv.at[at],
                device_id={"loop": device},
                device_id_type=pl.DeviceIdType.MESH,
            )

        core, side = partner(me, CORE), partner(me, mask)
        piece = rows // STEPS
        self.own_core = copy(0, 0, 1, core, 0, rows)
        self.direct = [copy(1 + i, 0, 2, side, i * piece, piece) for i in range(STEPS)]
        self.relay = [copy(1 + STEPS + i, 2, 3, core, i * piece, piece) for i in range(STEPS)]

    def start(self):
        for c in self.direct:
            c.start()
        self.own_core.start()

    def hand_on(self, i):
        self.direct[i].wait_recv()
        self.relay[i].start()

    def drain(self):
        for c in [self.own_core] + self.direct + self.relay:
            c.wait_send()


STEPS = 4
COPIES = 1 + 2 * STEPS
LAG = 2


class Line:
    def __init__(self, refs, owner, label_row, pieces):
        self.label_out, self.label_in, self.pair_in, self.table_out, self.table_in, self.hot, self.send, self.recv = refs
        self.label_row = label_row
        self.images = self.table_out.shape[1]
        self.pieces = pieces
        self.count = len(pieces)
        self.is_end = owner * (3 - owner) == 0
        self.is_inner = owner * (3 - owner) != 0
        self.inner = 1 + lax.div(owner, 3)
        self.end = (owner - 1) * 3
        self.owner, self.far_inner, self.far_end = owner, 3 - owner, 3 - self.end
        self.label_out[...] = jnp.broadcast_to(label_row, self.label_out.shape)
        self.labels = self.copy(0, self.label_out, self.label_in, self.inner)

    def copy(self, at, source, target, device):
        return pltpu.make_async_remote_copy(
            src_ref=source,
            dst_ref=target,
            send_sem=self.send.at[at],
            recv_sem=self.recv.at[at],
            device_id={"dp": device},
            device_id_type=pl.DeviceIdType.MESH,
        )

    def rows_copy(self, pair_v, k):
        part = (slice(None), pl.ds(*self.pieces[k]))
        return self.copy(1 + k, pair_v.at[part], self.pair_in.at[part], self.inner)

    def table_copy(self, slot, k):
        part = (slot, slice(None), pl.ds(*self.pieces[k]))
        device = (self.end, self.far_inner, self.far_end)[slot]
        at = 1 + (1 + slot) * self.count + k
        return self.copy(at, self.table_out.at[part], self.table_in.at[part], device)

    def mark(self, at, label_row, devices):
        images, rows = self.images, label_row.shape[1]
        ids = lax.broadcasted_iota(jnp.int32, (images, rows), 0).astype(jnp.float32)
        for i, device in enumerate(devices):
            hot = jnp.where(ids + (device * images).astype(jnp.float32) == label_row, 1.0, 0.0)
            self.hot[pl.ds((at + i) * images, images)] = hot.astype(jnp.bfloat16)

    def tables(self, at, count, values):
        hot = self.hot[pl.ds(at * self.images, count * self.images)]
        return jnp.dot(hot, values, preferred_element_type=jnp.float32)

    def prepare(self):
        @pl.when(self.is_end)
        def _():
            self.mark(0, self.label_row, [self.owner])

        @pl.when(self.is_inner)
        def _():
            devices = [self.far_inner, self.far_end, self.owner]
            self.mark(0, self.label_row, [self.end] + devices)
            self.labels.wait_recv()
            self.mark(4, self.label_in[pl.ds(0, 1)], devices)

    def send_labels(self):
        @pl.when(self.is_end)
        def _():
            self.labels.start()

    def ready(self, pair_v, k, d_image_ref):
        part = pl.ds(*self.pieces[k])

        @pl.when(self.is_end)
        def _():
            self.rows_copy(pair_v, k).start()
            d_image_ref[0, :, part] = self.tables(0, 1, pair_v[:, part])

        @pl.when(self.is_inner)
        def _():
            self.table_out[0, :, part] = self.tables(0, 1, pair_v[:, part]).astype(jnp.bfloat16)
            self.table_copy(0, k).start()

    def step(self, pair_v, k, d_image_ref):
        images = self.images
        part = pl.ds(*self.pieces[k])

        @pl.when(self.is_inner)
        def _():
            sums = self.tables(1, 3, pair_v[:, part])
            self.rows_copy(pair_v, k).wait_recv()
            sums = sums + self.tables(4, 3, self.pair_in[:, part])
            for slot in (1, 2):
                self.table_out[slot, :, part] = sums[(slot - 1) * images : slot * images].astype(jnp.bfloat16)
                self.table_copy(slot, k).start()
            d_image_ref[0, :, part] = sums[2 * images :]

    def last(self, pair_v, d_image_ref):
        @pl.when(self.is_end)
        def _():
            for k, piece in enumerate(self.pieces):
                part = pl.ds(*piece)
                self.table_copy(0, k).wait_recv()
                self.table_copy(2, k).wait_recv()
                d_image_ref[0, :, part] += (
                    self.table_in[0, :, part].astype(jnp.float32) + self.table_in[2, :, part].astype(jnp.float32)
                )
            self.labels.wait_send()
            for k in range(self.count):
                self.rows_copy(pair_v, k).wait_send()

        @pl.when(self.is_inner)
        def _():
            for k, piece in enumerate(self.pieces):
                part = pl.ds(*piece)
                self.table_copy(1, k).wait_recv()
                d_image_ref[0, :, part] += self.table_in[1, :, part].astype(jnp.float32)
            for k in range(self.count):
                for slot in range(3):
                    self.table_copy(slot, k).wait_send()


class Direct:
    def __init__(self, refs, owner, label_row, owners):
        self.table_out, self.table_in, self.send, self.recv = refs
        self.owner, self.label_row, self.owners = owner, label_row, owners

    def copy(self, apart):
        return pltpu.make_async_remote_copy(
            src_ref=self.table_out.at[apart],
            dst_ref=self.table_in.at[apart],
            send_sem=self.send.at[apart],
            recv_sem=self.recv.at[apart],
            device_id={"dp": lax.rem(self.owner + apart, self.owners)},
            device_id_type=pl.DeviceIdType.MESH,
        )

    def table(self, pair_v, apart):
        images, rows = self.table_out.shape[1], self.label_row.shape[1]
        first = lax.rem(self.owner + apart, self.owners) * images
        ids = lax.broadcasted_iota(jnp.int32, (images, rows), 0) + first
        onehot = jnp.where(ids.astype(jnp.float32) == self.label_row, 1.0, 0.0).astype(jnp.bfloat16)
        return jnp.dot(onehot, pair_v[...], preferred_element_type=jnp.float32)

    def send_labels(self):
        pass

    def prepare(self):
        pass

    def ready(self, pair_v, k, d_image_ref):
        if k + 1 < len(pieces_of(pair_v.shape[1])):
            return
        for apart in range(1, self.owners):
            self.table_out[apart] = self.table(pair_v, apart).astype(jnp.bfloat16)
            self.copy(apart).start()
        d_image_ref[0] = self.table(pair_v, 0)

    def step(self, pair_v, k, d_image_ref):
        pass

    def last(self, pair_v, d_image_ref):
        for apart in range(1, self.owners):
            self.copy(apart).wait_recv()
            d_image_ref[0] += self.table_in[apart].astype(jnp.float32)
        for apart in range(1, self.owners):
            self.copy(apart).wait_send()


def pieces_of(width):
    lanes = width // 128
    sizes = [1] + [2] * ((lanes - 3) // 2) + [1] * (2 - lanes % 2 + 1) if lanes > 3 else [1] * lanes
    return [(128 * sum(sizes[:i]), 128 * size) for i, size in enumerate(sizes)]


def kernel(
    owners,
    scale_ref,
    shift_ref,
    label_ref,
    image_ref,
    feat_ref,
    head_ref,
    d_feat_ref,
    d_image_ref,
    label_v,
    image_v,
    feat_v,
    head_v,
    xbuf,
    ybuf,
    x_weight,
    y_weight,
    unit_y_v,
    text_v,
    image_grad_v,
    d_pair_v,
    x_out,
    x_in,
    y_out,
    y_in,
    dots_out,
    dots_in,
    load_sem,
    x_send,
    x_recv,
    y_send,
    y_recv,
    px_send,
    px_recv,
    py_send,
    py_recv,
    *dp_refs,
):
    rows, width = image_v.shape
    me = lax.axis_index("loop")
    owner = lax.axis_index("dp")

    barrier = pltpu.get_barrier_semaphore()
    for mask in (CORE, NEAR, FAR):
        pl.semaphore_signal(
            barrier, inc=1, device_id={"loop": partner(me, mask)}, device_id_type=pl.DeviceIdType.MESH
        )
    for apart in range(1, owners):
        pl.semaphore_signal(
            barrier,
            inc=1,
            device_id={"dp": lax.rem(owner + apart, owners)},
            device_id_type=pl.DeviceIdType.MESH,
        )

    load_image = pltpu.make_async_copy(image_ref.at[0], image_v, load_sem.at[0])
    load_feat = pltpu.make_async_copy(feat_ref.at[0], feat_v, load_sem.at[1])
    load_head = pltpu.make_async_copy(head_ref, head_v, load_sem.at[2])
    load_label = pltpu.make_async_copy(label_ref, label_v, load_sem.at[3])
    load_label.start()
    load_image.start()
    load_feat.start()
    load_head.start()

    scale = scale_ref[0]
    shift = shift_ref[0]
    load_label.wait()
    label_row = label_v[...].astype(jnp.float32)
    label_grid = jnp.broadcast_to(label_row, (rows, rows))
    same = label_grid == label_grid.T

    xs = Spread(xbuf, x_send, x_recv, me, rows, NEAR)
    ys = Spread(ybuf, y_send, y_recv, me, rows, FAR)
    pieces = pieces_of(width)
    if owners == 4:
        sums = Line(dp_refs, owner, label_row, pieces)
    else:
        sums = Direct(dp_refs, owner, label_row, owners)

    def side_copy(source, target, send, recv, at, mask):
        return pltpu.make_async_remote_copy(
            src_ref=source,
            dst_ref=target,
            send_sem=send.at[at],
            recv_sem=recv.at[at],
            device_id={"loop": partner(me, mask)},
            device_id_type=pl.DeviceIdType.MESH,
        )

    columns = [(slice(None), pl.ds(*piece)) for piece in pieces]
    x_parts = [side_copy(x_out.at[c], x_in.at[c], px_send, px_recv, k, NEAR) for k, c in enumerate(columns)]
    y_parts = [side_copy(y_out.at[c], y_in.at[c], py_send, py_recv, k, FAR) for k, c in enumerate(columns)]
    dots_copy = side_copy(dots_out, dots_in, px_send, px_recv, len(pieces), NEAR)

    load_image.wait()
    image = image_v[...].astype(jnp.float32)
    inv_x = lax.rsqrt(jnp.sum(image * image, axis=-1, keepdims=True) + EPS)
    xbuf[pl.ds(0, rows)] = (image * inv_x).astype(jnp.bfloat16)

    pl.semaphore_wait(barrier, 3 + owners - 1)
    xs.start()
    sums.send_labels()

    load_feat.wait()
    load_head.wait()
    text_pre = jnp.dot(feat_v[...], head_v[...], preferred_element_type=jnp.float32)
    inv_y = lax.rsqrt(jnp.sum(text_pre * text_pre, axis=-1, keepdims=True) + EPS)
    unit_y = text_pre * inv_y
    ybuf[pl.ds(0, rows)] = unit_y.astype(jnp.bfloat16)
    ys.start()
    unit_y_v[...] = unit_y

    def weights(mine, row, other, block, blocks, weight):
        dots = lax.dot_general(
            mine[pl.ds(row * 2 * rows, rows)],
            other[pl.ds(block * rows, blocks * rows)],
            NT,
            preferred_element_type=jnp.float32,
        )
        logits = scale * dots + shift
        if row == 0 and block == 0:
            flip = jnp.concatenate([same, jnp.zeros_like(same)], axis=1)
            value = jax.nn.sigmoid(jnp.where(flip, -logits, logits))
            value = jnp.where(flip, -value, value)
        else:
            value = jax.nn.sigmoid(logits)
        value = value.astype(jnp.bfloat16)
        weight[pl.ds(row * rows, rows), pl.ds(block * rows, blocks * rows)] = value
        return value.astype(jnp.float32) * dots

    def product(weight, row, buf, column):
        return jnp.dot(weight[pl.ds(row * rows, rows)], buf[column], preferred_element_type=jnp.float32)

    everything = (slice(None), slice(None))

    ys.own_core.wait_recv()
    xs.own_core.wait_recv()
    own_dots = weights(xbuf, 0, ybuf, 0, 2, x_weight)
    ys.hand_on(0)
    xs.hand_on(0)
    weights(ybuf, 0, xbuf, 0, 2, y_weight)
    for i in range(1, STEPS):
        xs.hand_on(i)
        ys.hand_on(i)
    near_dots = weights(xbuf, 1, ybuf, 0, 2, x_weight)

    for c in ys.relay:
        c.wait_recv()
    near_dots = jnp.sum(near_dots + weights(xbuf, 1, ybuf, 2, 2, x_weight), axis=-1, keepdims=True)
    dots_out[...] = jnp.broadcast_to(near_dots, (rows, rows)).T[:8]
    dots_copy.start()
    for first in range(0, len(pieces), 2):
        pair = pieces[first : first + 2]
        part = (slice(None), pl.ds(pair[0][0], sum(size for _, size in pair)))
        x_out[part] = product(x_weight, 1, ybuf, part).astype(jnp.bfloat16)
        for c in x_parts[first : first + 2]:
            c.start()

    own_dots = jnp.sum(own_dots + weights(xbuf, 0, ybuf, 2, 2, x_weight), axis=-1, keepdims=True)
    image_grad_v[...] = product(x_weight, 0, ybuf, everything)
    sums.prepare()
    dots_copy.wait_recv()
    there = jnp.broadcast_to(dots_in[pl.ds(0, 1)], (rows, rows)).T[:, :1]
    along = scale * (own_dots + there)

    def far_texts():
        for c in xs.relay:
            c.wait_recv()
        weights(ybuf, 1, xbuf, 0, 4, y_weight)
        y_out[...] = product(y_weight, 1, xbuf, everything).astype(jnp.bfloat16)
        for c in y_parts:
            c.start()

    def own_texts():
        weights(ybuf, 0, xbuf, 2, 2, y_weight)
        text_v[...] = product(y_weight, 0, xbuf, everything)

    fill = {1: far_texts, len(pieces) - 3: own_texts}
    for k, c in enumerate(columns):
        unit_x = image_v[c].astype(jnp.float32) * inv_x
        x_parts[k].wait_recv()
        grad = scale * (image_grad_v[c] + x_in[c].astype(jnp.float32))
        d_pair_v[c] = ((grad - unit_x * along) * inv_x).astype(jnp.bfloat16)
        sums.ready(d_pair_v, k, d_image_ref)
        if k in fill:
            fill[k]()
        if k >= LAG:
            sums.step(d_pair_v, k - LAG, d_image_ref)

    for k in range(len(pieces) - LAG, len(pieces)):
        sums.step(d_pair_v, k, d_image_ref)
    for c in y_parts:
        c.wait_recv()
    grad = scale * (text_v[...] + y_in[...].astype(jnp.float32))
    unit_y = unit_y_v[...]
    d_text = (grad - unit_y * jnp.sum(unit_y * grad, axis=-1, keepdims=True)) * inv_y
    d_feat_ref[0] = lax.dot_general(
        d_text.astype(jnp.bfloat16), head_v[...], NT, preferred_element_type=jnp.float32
    )

    sums.last(d_pair_v, d_image_ref)
    xs.drain()
    ys.drain()
    for c in x_parts + y_parts + [dots_copy]:
        c.wait_send()


def store(feat_v, image_v, d_feat_ref, d_image_ref, sem):
    feat = pltpu.make_async_copy(feat_v, d_feat_ref, sem.at[0])
    image = pltpu.make_async_copy(image_v, d_image_ref, sem.at[1])
    feat.start()
    image.start()
    feat.wait()
    image.wait()


def shards(owners, image_raw, text_feat, text_head, image_of_pair, logit_scale, logit_bias):
    _, rows, width = image_raw.shape
    depth = text_head.shape[0]
    images = rows // 2
    hbm = pl.BlockSpec(memory_space=pltpu.HBM)
    scalar = pl.BlockSpec(memory_space=pltpu.SMEM)
    vmem = pl.BlockSpec(memory_space=pltpu.VMEM)
    dma = pltpu.SemaphoreType.DMA
    count = len(pieces_of(width))
    if owners == 4:
        dp_scratch = [
            pltpu.VMEM((8, rows), jnp.float32),
            pltpu.VMEM((8, rows), jnp.float32),
            pltpu.VMEM((rows, width), jnp.bfloat16),
            pltpu.VMEM((3, images, width), jnp.bfloat16),
            pltpu.VMEM((3, images, width), jnp.bfloat16),
            pltpu.VMEM((7 * images, rows), jnp.bfloat16),
            dma((1 + 4 * count,)),
            dma((1 + 4 * count,)),
        ]
    else:
        dp_scratch = [
            pltpu.VMEM((owners, images, width), jnp.bfloat16),
            pltpu.VMEM((owners, images, width), jnp.bfloat16),
            dma((owners,)),
            dma((owners,)),
        ]
    results = (
        jax.ShapeDtypeStruct((1, rows, depth), jnp.float32),
        jax.ShapeDtypeStruct((1, images, width), jnp.float32),
    )
    gradients = pl.pallas_call(
        functools.partial(kernel, owners),
        out_shape=results,
        in_specs=[scalar, scalar, hbm, hbm, hbm, hbm],
        out_specs=(vmem, vmem),
        scratch_shapes=[
            pltpu.VMEM((1, rows), jnp.int32),
            pltpu.VMEM((rows, width), jnp.bfloat16),
            pltpu.VMEM((rows, depth), jnp.bfloat16),
            pltpu.VMEM((depth, width), jnp.bfloat16),
            pltpu.VMEM((4 * rows, width), jnp.bfloat16),
            pltpu.VMEM((4 * rows, width), jnp.bfloat16),
            pltpu.VMEM((2 * rows, 4 * rows), jnp.bfloat16),
            pltpu.VMEM((2 * rows, 4 * rows), jnp.bfloat16),
            pltpu.VMEM((rows, width), jnp.float32),
            pltpu.VMEM((rows, width), jnp.float32),
            pltpu.VMEM((rows, width), jnp.float32),
            pltpu.VMEM((rows, width), jnp.bfloat16),
            pltpu.VMEM((rows, width), jnp.bfloat16),
            pltpu.VMEM((rows, width), jnp.bfloat16),
            pltpu.VMEM((rows, width), jnp.bfloat16),
            pltpu.VMEM((rows, width), jnp.bfloat16),
            pltpu.VMEM((8, rows), jnp.float32),
            pltpu.VMEM((8, rows), jnp.float32),
            dma((4,)),
            dma((COPIES,)),
            dma((COPIES,)),
            dma((COPIES,)),
            dma((COPIES,)),
            dma((count + 1,)),
            dma((count + 1,)),
            dma((count,)),
            dma((count,)),
            *dp_scratch,
        ],
        compiler_params=pltpu.CompilerParams(
            collective_id=0, has_side_effects=True, vmem_limit_bytes=32 * 1024 * 1024
        ),
    )(
        logit_scale.reshape((1,)),
        logit_bias.reshape((1,)),
        *(
            pltpu.with_memory_space_constraint(a, pltpu.HBM)
            for a in (image_of_pair, image_raw, text_feat, text_head)
        ),
    )
    return pl.pallas_call(
        store,
        out_shape=results,
        in_specs=[vmem, vmem],
        out_specs=(hbm, hbm),
        scratch_shapes=[dma((2,))],
        compiler_params=pltpu.CompilerParams(vmem_limit_bytes=4 * 1024 * 1024),
    )(*gradients)


def solution(mesh):
    placed = (P("dp", "loop", None), P("dp", "loop", None), P(), P("dp", "loop"), P(), P())
    return jax.shard_map(
        functools.partial(shards, mesh.shape["dp"]),
        mesh=mesh,
        in_specs=placed,
        out_specs=(P("dp", "loop", None), P("loop", "dp", None)),
        check_vma=False,
    )
```
